256 devices in a mesh: mesh: 16 (over x_hi, y, core), four: 16 (over x_lo, z).
Axes of the slice: x: 4 (x_hi: 2, x_lo: 2; x = x_hi * 2 + x_lo), y: 4, z: 8, core: 2. Of those that a mesh axis runs over, the one named last changes fastest.
Arguments:
- adj_modes: float32 [3, 256, 64, 4096], P(None, 'four', None, 'mesh'), may hold values from -1 to 1
- base_flow: bfloat16 [12, 256, 64, 4096], P(None, None, 'four', 'mesh'), may hold values from -6 to 6
- geometry: float32 [4, 64, 4096], P(None, None, 'mesh'), may hold values from -1 to 1
- mass: float32 [64, 4096], P(None, 'mesh'), may hold values from 0.2 to 2
- connect: int32 [64, 4096], P(None, 'mesh'), may hold values from 0 to 12824, as said below
- edge_nodes: int32 [16, 2, 225], P('mesh'), may hold values from 0 to 12824, as said below
Outputs:
- adj_next: float32 [3, 256, 64, 4096], P(None, 'four', None, 'mesh')
The draws below stay inside these ranges and needn't reach their ends.
Inputs may be any that keep to these rules, and one draw needn't show every extreme that they name: `connect`: columns p * 256 to (p + 1) * 256 - 1 form partition p. Each partition numbers its 12825 nodes from 0; element nodes at the same place share an id, and every id is used. edge_nodes[p, 1] lists the ids of partition p's nodes that coincide with nodes of partition p + 1 (mod 16), in the same order in which edge_nodes[p + 1, 0] lists them; the two lists of a partition are disjoint, and no other node is shared between partitions.
All inputs are finite; a program needn't handle non-finite values.
Results may differ from the reference program's by a relative error of at most 0.0003.
Values sent between devices are 32-bit elements; how exact they have to be, the bound alone decides.
A program may use at most 128 MiB of HBM per device.

```python
import math
import jax
import jax.numpy as jnp
from jax import lax

NP = 8
NODES = 64
PLANES = 256
ER = 32
EA = 8
E_DEV = 256
ELEMS = 4096
UNIQUE = 12825
N_MESH = 16


def mesh_tables(key):
    radial_n = (NP - 1) * ER + 1
    azimuth_n = (NP - 1) * EA + 1

    def one_part(part_index):
        part_key = jax.random.fold_in(key, part_index)
        node_perm = jax.random.permutation(jax.random.fold_in(part_key, 1), radial_n * azimuth_n).astype(jnp.int32)
        elem_perm = jax.random.permutation(jax.random.fold_in(part_key, 2), ER * EA).astype(jnp.int32)
        elem_radial = elem_perm // EA
        elem_azimuth = elem_perm % EA
        node_index = jnp.arange(NP * NP, dtype=jnp.int32)
        first_dir = node_index // NP
        second_dir = node_index % NP
        radial_pos = (NP - 1) * elem_radial[None, :] + first_dir[:, None]
        azimuth_pos = (NP - 1) * elem_azimuth[None, :] + second_dir[:, None]
        conn_part = node_perm[radial_pos * azimuth_n + azimuth_pos]
        radial_all = jnp.arange(radial_n, dtype=jnp.int32)
        lower = node_perm[radial_all * azimuth_n]
        upper = node_perm[radial_all * azimuth_n + azimuth_n - 1]
        return (conn_part, jnp.stack([lower, upper]))
    conn_all, edge_all = jax.vmap(one_part)(jnp.arange(N_MESH, dtype=jnp.int32))
    conn_all = conn_all.transpose(1, 0, 2).reshape(NP * NP, N_MESH * ER * EA)
    return (conn_all, edge_all)


def draw_connect(key, part):
    return mesh_tables(key)[0]


def draw_edge_nodes(key, part):
    return mesh_tables(key)[1]


def shard_levels(rng, shape, cuts, least, high):
    gain, own = 1.0, jax.random.fold_in(rng, 6)
    for dim, shards_of in cuts:
        draws = jnp.exp(jax.random.uniform(jax.random.fold_in(own, dim), (shards_of,), jnp.float32, least / len(cuts), high / len(cuts)))
        gain = gain * jnp.repeat(draws, shape[dim] // shards_of).reshape([-1 if axis == dim else 1 for axis in range(len(shape))])
    return gain


def gaussian(rng, extent, scale, bound, cuts=(), kind=jnp.bfloat16):
    array = scale * jax.random.normal(rng, extent, jnp.float32)
    if cuts:
        array = array * shard_levels(rng, extent, cuts, -0.22, 0.18)
    return jnp.clip(array, -bound, bound).astype(kind)


def setup_inputs(seed: int = 0) -> dict:
    streams_of = jax.random.split(jax.random.key(seed), 7)
    return {
        "adj_modes": gaussian(streams_of[0], (3, PLANES, NODES, ELEMS), (PLANES ** -0.5), 1.0, ((1, 16), (3, 16)), jnp.float32),
        "base_flow": gaussian(streams_of[1], (12, PLANES, NODES, ELEMS), 1.0, 6.0, ((2, 16), (3, 16))),
        "geometry": gaussian(streams_of[2], (4, NODES, ELEMS), 0.2, 1.0, ((2, 16),), jnp.float32),
        "mass": jnp.clip(jnp.exp(math.log(2.0) - 2.3025851 * jax.random.uniform(streams_of[3], (NODES, ELEMS), jnp.float32) ** shard_levels(streams_of[3], (NODES, ELEMS), ((1, 16),), -0.2, 0.2)), 0.2, 2.0),
        "connect": draw_connect(jax.random.fold_in(streams_of[6], 71), 0),
        "edge_nodes": draw_edge_nodes(jax.random.fold_in(streams_of[6], 71), 0),
    }


STEP_SIZE = 0.1
HIGH = lax.Precision.HIGHEST


def legendre_values(degree, point):
    before = 1.0
    current = point
    for order in range(1, degree):
        after = ((2 * order + 1) * point * current - order * before) / (order + 1)
        before = current
        current = after
    return current, before


def gll_derivative(points_n):
    degree = points_n - 1
    points = []
    for index in range(points_n):
        point = -math.cos(math.pi * index / degree)
        for sweep in range(100):
            top_val, below_val = legendre_values(degree, point)
            point = point - (point * top_val - below_val) / (points_n * top_val)
        points.append(point)
    values = [legendre_values(degree, point)[0] for point in points]
    deriv_rows = []
    for row_index in range(points_n):
        row_vals = []
        for col_index in range(points_n):
            if row_index != col_index:
                row_vals.append(values[row_index] / (values[col_index] * (points[row_index] - points[col_index])))
            else:
                row_vals.append(0.0)
        deriv_rows.append(row_vals)
    deriv_rows[0][0] = -degree * (degree + 1) / 4.0
    deriv_rows[degree][degree] = degree * (degree + 1) / 4.0
    deriv_table = jnp.asarray(deriv_rows, jnp.float32)
    identity = jnp.eye(points_n, dtype=jnp.float32)
    return jnp.kron(deriv_table, identity), jnp.kron(identity, deriv_table)


def plane_tables(planes):
    plane_idx = jnp.arange(planes, dtype=jnp.int32)
    wave_idx = plane_idx // 2
    phase = ((plane_idx[:, None] * wave_idx[None, :]) % planes).astype(jnp.float32) * (2.0 * math.pi / planes)
    is_sine = (plane_idx % 2) == 1
    synth = jnp.where(is_sine[None, :], jnp.sin(phase), jnp.cos(phase))
    alternate = (1 - 2 * (plane_idx % 2)).astype(jnp.float32)
    synth = synth.at[:, 1].set(alternate)
    scales = jnp.where(wave_idx == 0, 1.0 / planes, 2.0 / planes).astype(jnp.float32)
    analysis = synth.T * scales[:, None]
    return synth, analysis


def axial(coef, wave):
    pairs = coef.reshape(coef.shape[0], coef.shape[1] // 2, 2, coef.shape[2], coef.shape[3])
    factor = wave[None, :, None, None]
    return jnp.stack([factor * pairs[:, :, 1], -factor * pairs[:, :, 0]], axis=2).reshape(coef.shape)


def gradients(coef, geometry, deriv_r, deriv_s):
    along_r = jnp.einsum('mn,fpne->fpme', deriv_r, coef, precision=HIGH)
    along_s = jnp.einsum('mn,fpne->fpme', deriv_s, coef, precision=HIGH)
    grad_x = geometry[0] * along_r + geometry[1] * along_s
    grad_y = geometry[2] * along_r + geometry[3] * along_s
    return grad_x, grad_y


def advect(physical, base):
    pieces = []
    for component in range(3):
        total = jnp.zeros(physical.shape[1:], jnp.float32)
        for direction in range(3):
            total = total - base[direction].astype(jnp.float32) * physical[3 + 3 * direction + component] + physical[direction] * base[3 + 3 * component + direction].astype(jnp.float32)
        pieces.append(total)
    return jnp.stack(pieces)


def take_cols(table_rows, node_ids):
    return table_rows[:, node_ids]


def put_cols(table_rows, node_ids, new_vals):
    return table_rows.at[:, node_ids].set(new_vals)


def reference(adj_modes, base_flow, geometry, mass, connect, edge_nodes):
    deriv_r, deriv_s = gll_derivative(NP)
    synth, analysis = plane_tables(PLANES)
    wave = jnp.arange(PLANES // 2, dtype=jnp.int32).astype(jnp.float32) * (2.0 / PLANES)

    def one_part(part_index):
        start = (part_index * E_DEV).astype(jnp.int32)
        coef = lax.dynamic_slice_in_dim(adj_modes, start, E_DEV, 3)
        base = lax.dynamic_slice_in_dim(base_flow, start, E_DEV, 3)
        geo_part = lax.dynamic_slice_in_dim(geometry, start, E_DEV, 2)
        weights = lax.dynamic_slice_in_dim(mass, start, E_DEV, 1)
        node_ids = lax.dynamic_slice_in_dim(connect, start, E_DEV, 1).reshape(-1)
        grad_x, grad_y = gradients(coef, geo_part, deriv_r, deriv_s)
        grad_z = axial(coef, wave)
        fields = jnp.concatenate([coef, grad_x, grad_y, grad_z])
        physical = jnp.einsum('jm,fmne->fjne', synth, fields, precision=HIGH)
        forcing = advect(physical, base)
        forcing_modes = jnp.einsum('mj,fjne->fmne', analysis, forcing, precision=HIGH)
        weighted = weights * (coef + STEP_SIZE * forcing_modes)
        rows = jnp.concatenate([weighted.reshape(3 * PLANES, -1), weights.reshape(1, -1)])
        return jnp.zeros((rows.shape[0], UNIQUE), jnp.float32).at[:, node_ids].add(rows)

    summed = lax.map(one_part, jnp.arange(N_MESH, dtype=jnp.int32))
    lower = edge_nodes[:, 0]
    upper = edge_nodes[:, 1]
    low_vals = jax.vmap(take_cols)(summed, lower)
    high_vals = jax.vmap(take_cols)(summed, upper)
    new_low = low_vals + jnp.roll(high_vals, 1, axis=0)
    new_high = high_vals + jnp.roll(low_vals, -1, axis=0)
    summed = jax.vmap(put_cols)(summed, lower, new_low)
    summed = jax.vmap(put_cols)(summed, upper, new_high)
    conn_parts = connect.reshape(NODES, N_MESH, E_DEV).transpose(1, 0, 2).reshape(N_MESH, -1)
    spread = jax.vmap(take_cols)(summed, conn_parts)
    result = spread[:, :-1] / spread[:, -1:]
    result = result.reshape(N_MESH, 3, PLANES, NODES, E_DEV).transpose(1, 2, 3, 0, 4)
    return result.reshape(3, PLANES, NODES, ELEMS)
```

```python
import functools
import math

import jax
import jax.numpy as jnp
import numpy as np
from jax import lax
from jax.experimental import pallas as pl
from jax.experimental.pallas import tpu as pltpu
from jax.sharding import PartitionSpec as P

NP = 8
NODES = 64
PLANES = 256
UNIQUE = 12825
E_DEV = 256
POINTS = NODES * E_DEV
EXTRA = POINTS - UNIQUE
LIST_ROWS = (EXTRA + 1023) // 1024 * 8
RIM = 225
RIM_PAD = 512
HALVES = 2
LANES = E_DEV // HALVES
GROUP = 16
COEFS = PLANES // GROUP
STEP_SIZE = 0.1
HIGH = lax.Precision.HIGHEST
MESH = pl.DeviceIdType.MESH
VMEM_LIMIT = 60 * 2**20


def legendre_values(degree, point):
    before = 1.0
    current = point
    for order in range(1, degree):
        after = ((2 * order + 1) * point * current - order * before) / (order + 1)
        before = current
        current = after
    return (current, before)


def gll_derivative(points_n):
    degree = points_n - 1
    points = []
    for index in range(points_n):
        point = -math.cos(math.pi * index / degree)
        for sweep in range(100):
            top_val, below_val = legendre_values(degree, point)
            point = point - (point * top_val - below_val) / (points_n * top_val)
        points.append(point)
    values = [legendre_values(degree, point)[0] for point in points]
    rows = [
        [
            0.0 if r == c else values[r] / (values[c] * (points[r] - points[c]))
            for c in range(points_n)
        ]
        for r in range(points_n)
    ]
    rows[0][0] = -degree * (degree + 1) / 4.0
    rows[degree][degree] = degree * (degree + 1) / 4.0
    return np.asarray(rows, np.float32)


def plane_tables():
    plane = np.arange(PLANES)
    wave = plane // 2
    phase = (plane[:, None] * wave[None, :] % PLANES) * (2.0 * math.pi / PLANES)
    synth = np.where(plane[None, :] % 2 == 1, np.sin(phase), np.cos(phase))
    synth[:, 1] = 1 - 2 * (plane % 2)
    scales = np.where(wave == 0, 1.0 / PLANES, 2.0 / PLANES)
    analysis = synth.T * scales[:, None]
    number = wave * (2.0 / PLANES)
    axial = np.zeros((PLANES, PLANES))
    axial[plane[::2], plane[1::2]] = number[::2]
    axial[plane[1::2], plane[::2]] = -number[1::2]
    both = np.concatenate([synth, synth @ axial])
    return both.astype(np.float32), (STEP_SIZE * analysis).astype(np.float32)


def step_kernel(
    u_ref, base_ref, geo_ref, mass_ref, synth_ref, anal_ref, table_ref,
    ut, along, rows, slopes, base, stage, inputs, fields, forcing, back, returned, table,
    row_send, relay_send, slope_send, back_send, row_recv, slope_recv, back_recv,
    own_sem, stage_sem, table_sem,
):
    deriv = gll_derivative(NP)
    me = lax.axis_index("four")
    x, z = me // 8, me % 8
    odd = z % 2
    sign = 1 - 2 * odd
    partner = x * 8 + z + sign

    def remote(src, dst, send, recv, to):
        return pltpu.make_async_remote_copy(
            src_ref=src, dst_ref=dst, send_sem=send, recv_sem=recv,
            device_id={"four": to}, device_id_type=MESH,
        )

    def source(dx, k):
        return ((x + dx) % 2) * 8 + (z - sign * k + 8) % 8

    def target(dx, k):
        off = (0, 2, -1, -3)[k]
        return ((x + dx) % 2) * 8 + (z + sign * off + 8) % 8

    def pair(dev):
        return pl.multiple_of((dev // 2) * 8, 8)

    def stage_copy(f):
        return pltpu.make_async_copy(base_ref.at[f], stage.at[f % 2], stage_sem.at[f % 2])

    def turn(h):
        def block(t, _):
            c = t // 8
            i = pl.multiple_of((t % 8) * 8, 8)
            ut[h, c, pl.ds(i, 8)] = jnp.swapaxes(u_ref[c, :, pl.ds(i, 8), pl.ds(h * LANES, LANES)], 0, 1)
            return 0
        lax.fori_loop(0, 24, block, 0)

    def differentiate(h):
        def block(t, _):
            c, j = t // 8, t % 8
            vals = [ut[h, c, 8 * i + j] for i in range(8)]
            for i in range(8):
                total = vals[0] * float(deriv[i, 0])
                for k in range(1, 8):
                    total = total + vals[k] * float(deriv[i, k])
                along[h, c, 8 * i + j] = total
            return 0
        lax.fori_loop(0, 24, block, 0)

    def row_copy(h, dx, k):
        to = target(dx, k)
        return remote(ut.at[h, :, pl.ds(pair(to), 8)], rows.at[h, me], row_send.at[h, dx * 4 + k], row_recv.at[h, me], to)

    def own_relay(h):
        return remote(ut.at[h, :, pl.ds(pair(me), 8)], rows.at[h, me], relay_send.at[h, 0], row_recv.at[h, me], partner)

    def relay(h, dx, k):
        src = source(dx, k)
        return remote(rows.at[h, src], rows.at[h, src], relay_send.at[h, dx * 4 + k], row_recv.at[h, src], partner)

    def far_source(dx, k):
        return ((x + dx) % 2) * 8 + (z + sign + sign * k + 8) % 8

    def row_wait(h, src):
        remote(rows.at[h, src], rows.at[h, src], relay_send.at[h, 0], row_recv.at[h, src], partner).wait_recv()

    def slope_copy(h, t):
        to = (me + t) % GROUP
        return remote(
            along.at[h, :, pl.ds(to * 4, 4)], slopes.at[h, me], slope_send.at[h, t], slope_recv.at[h, me], to
        )

    def slope_wait(h, t):
        src = (me + t) % GROUP
        remote(slopes.at[h, src], slopes.at[h, src], slope_send.at[h, t], slope_recv.at[h, src], src).wait_recv()

    def back_copy(h, t):
        to = (me + t) % GROUP
        return remote(back.at[h, to], returned.at[h, me], back_send.at[h, t], back_recv.at[h, me], to)

    def back_wait(h, src):
        remote(returned.at[h, src], returned.at[h, src], back_send.at[h, 0], back_recv.at[h, src], partner).wait_recv()

    def own_copies(h):
        return (
            pltpu.make_async_copy(ut.at[h, :, pl.ds(pair(me), 8)], rows.at[h, me], own_sem.at[h, 0]),
            pltpu.make_async_copy(along.at[h, :, pl.ds(me * 4, 4)], slopes.at[h, me], own_sem.at[h, 1]),
        )

    def own_back(h):
        return pltpu.make_async_copy(back.at[h, me], returned.at[h, me], own_sem.at[h, 2])

    NEAR = [(1, 0), (0, 1), (1, 1), (0, 2), (1, 2), (0, 3), (1, 3)]
    SENT = [(0, 3), (1, 3), (0, 1), (1, 1), (0, 2), (1, 2), (1, 0)]

    def each(fn):
        def go(t, _):
            fn(t)
            return 0
        lax.fori_loop(1, GROUP, go, 0)

    def send_rows(h):
        for dx, k in SENT:
            row_copy(h, dx, k).start()
        own_relay(h).start()

    def send_slopes(h):
        each(lambda t: slope_copy(h, t).start())

    def relays(h):
        for dx, k in NEAR:
            row_wait(h, source(dx, k))
            relay(h, dx, k).start()

    def compute(h):
        for copy in own_copies(h):
            copy.wait()
        for k in range(4):
            for dx in range(2):
                row_wait(h, far_source(dx, k))
        each(lambda t: slope_wait(h, t))

        def gather(s, _):
            at = pl.ds(pl.multiple_of(s * COEFS, COEFS), COEFS)
            for c in range(3):
                line = [rows[h, s, c, j] for j in range(8)]
                for n in range(4):
                    total = None
                    for k in range(8):
                        term = line[k] * jnp.where(odd == 1, float(deriv[4 + n, k]), float(deriv[n, k]))
                        total = term if total is None else total + term
                    inputs[n, at, pl.ds(c * LANES, LANES)] = jnp.where(odd == 1, line[4 + n], line[n])
                    inputs[n, at, pl.ds((3 + c) * LANES, LANES)] = total
                    inputs[n, at, pl.ds((6 + c) * LANES, LANES)] = slopes[h, s, c, n]
            return 0
        lax.fori_loop(0, GROUP, gather, 0)

        def node(n, _):
            fields[:, 0 : 9 * LANES] = jnp.dot(
                synth_ref[0:PLANES], inputs[n], precision=HIGH, preferred_element_type=jnp.float32
            )
            fields[:, 9 * LANES : 12 * LANES] = jnp.dot(
                synth_ref[PLANES : 2 * PLANES], inputs[n, :, 0 : 3 * LANES],
                precision=HIGH, preferred_element_type=jnp.float32,
            )
            geo = [geo_ref[g, n, :, pl.ds(h * LANES, LANES)] for g in range(4)]

            def planes(p, _):
                at = pl.ds(pl.multiple_of(p * 16, 16), 16)
                flow = [base[f, n, at, pl.ds(h * LANES, LANES)].astype(jnp.float32) for f in range(12)]
                get = lambda f: fields[at, f * LANES : (f + 1) * LANES]
                on_r = flow[0] * geo[0] + flow[1] * geo[2]
                on_s = flow[0] * geo[1] + flow[1] * geo[3]
                vel = [get(c) for c in range(3)]
                for c in range(3):
                    total = vel[0] * flow[3 + 3 * c] + vel[1] * flow[4 + 3 * c] + vel[2] * flow[5 + 3 * c]
                    total = total - on_r * get(6 + c) - on_s * get(3 + c) - flow[2] * get(9 + c)
                    forcing[at, c * LANES : (c + 1) * LANES] = total
                return 0
            lax.fori_loop(0, PLANES // 16, planes, 0)
            modes = jnp.dot(anal_ref[...], forcing[...], precision=HIGH, preferred_element_type=jnp.float32)
            for c in range(3):
                back[h, :, c, n] = modes[:, c * LANES : (c + 1) * LANES].reshape(GROUP, COEFS, LANES)
            return 0
        lax.fori_loop(0, 4, node, 0)

    def table_copy(h, s):
        at = pl.ds(pl.multiple_of((h * NODES + 4 * s) * LANES, 4 * LANES), 4 * LANES)
        return pltpu.make_async_copy(table.at[at], table_ref.at[at], table_sem.at[h, s])

    def finish(h, s):
        for n in range(4):
            at = 4 * s + n
            weight = mass_ref[at, :, pl.ds(h * LANES, LANES)]
            parts = [(ut[h, c, at] + returned[h, s, c, n]) * weight for c in range(3)]
            parts.append(jnp.broadcast_to(weight, (8, LANES)))
            parts.append(jnp.zeros((128 - 56, LANES), jnp.float32))
            begin = pl.multiple_of((h * NODES + at) * LANES, LANES)
            table[pl.ds(begin, LANES)] = jnp.concatenate(parts).T
        table_copy(h, s).start()

    stage_copy(0).start()
    stage_copy(1).start()
    barrier = pltpu.get_barrier_semaphore()
    each(lambda t: pl.semaphore_signal(barrier, inc=1, device_id={"four": (me + t) % GROUP}, device_id_type=MESH))
    turn(0)
    pl.semaphore_wait(barrier, GROUP - 1)
    send_rows(0)
    differentiate(0)
    send_slopes(0)
    for copy in own_copies(0):
        copy.start()
    turn(1)
    differentiate(1)
    for copy in own_copies(1):
        copy.start()

    for f in range(12):
        stage_copy(f).wait()

        def move(t, _):
            p = pl.multiple_of(t * 64, 64)
            block = stage[f % 2, pl.ds(p, 64)].astype(jnp.float32)
            base[f, :, pl.ds(p, 64), :] = jnp.swapaxes(block, 0, 1).astype(jnp.bfloat16)
            return 0
        lax.fori_loop(0, 4, move, 0)
        if f + 2 < 12:
            stage_copy(f + 2).start()

    relays(0)
    send_rows(1)
    send_slopes(1)
    compute(0)
    own_back(0).start()
    relays(1)
    each(lambda t: back_copy(0, t).start())
    compute(1)
    own_back(1).start()
    each(lambda t: back_copy(1, t).start())

    for h in range(HALVES):
        own_back(h).wait()
        finish(h, me)

        def arrive(t, _):
            src = (me + t) % GROUP
            back_wait(h, src)
            finish(h, src)
            return 0
        lax.fori_loop(1, GROUP, arrive, 0)

    for h in range(HALVES):
        for dx, k in SENT:
            row_copy(h, dx, k).wait_send()
        own_relay(h).wait_send()
        for dx, k in NEAR:
            relay(h, dx, k).wait_send()
        each(lambda t: slope_copy(h, t).wait_send())
        each(lambda t: back_copy(h, t).wait_send())

        def drained(s, _):
            table_copy(h, s).wait()
            return 0
        lax.fori_loop(0, GROUP, drained, 0)


def step(u, base, geo, mass):
    synth, anal = plane_tables()
    vmem = pl.BlockSpec(memory_space=pltpu.VMEM)
    hbm = pl.BlockSpec(memory_space=pl.ANY)
    f32 = jnp.float32
    dma = pltpu.SemaphoreType.DMA
    return pl.pallas_call(
        step_kernel,
        out_shape=jax.ShapeDtypeStruct((POINTS, 128), f32),
        in_specs=[vmem, hbm, vmem, vmem, vmem, vmem],
        out_specs=hbm,
        scratch_shapes=[
            pltpu.VMEM((HALVES, 3, NODES, COEFS, LANES), f32),
            pltpu.VMEM((HALVES, 3, NODES, COEFS, LANES), f32),
            pltpu.VMEM((HALVES, GROUP, 3, 8, COEFS, LANES), f32),
            pltpu.VMEM((HALVES, GROUP, 3, 4, COEFS, LANES), f32),
            pltpu.VMEM((12, 4, PLANES, E_DEV), jnp.bfloat16),
            pltpu.VMEM((2, PLANES, 4, E_DEV), jnp.bfloat16),
            pltpu.VMEM((4, PLANES, 9 * LANES), f32),
            pltpu.VMEM((PLANES, 12 * LANES), f32),
            pltpu.VMEM((PLANES, 3 * LANES), f32),
            pltpu.VMEM((HALVES, GROUP, 3, 4, COEFS, LANES), f32),
            pltpu.VMEM((HALVES, GROUP, 3, 4, COEFS, LANES), f32),
            pltpu.VMEM((POINTS, 128), f32),
            dma((HALVES, 8)), dma((HALVES, 8)), dma((HALVES, GROUP)), dma((HALVES, GROUP)),
            dma((HALVES, GROUP)), dma((HALVES, GROUP)), dma((HALVES, GROUP)),
            dma((HALVES, 3)), dma((2,)), dma((HALVES, GROUP)),
        ],
        compiler_params=pltpu.CompilerParams(
            collective_id=0, has_side_effects=True, vmem_limit_bytes=VMEM_LIMIT
        ),
        name="step",
    )(u, base, geo, mass, jnp.asarray(synth), jnp.asarray(anal))


def lists_block(n, ids_ref, state):
    counts, firsts, lists, used = state
    bf, f32 = jnp.bfloat16, jnp.float32
    width = E_DEV

    def iota(shape, dim):
        return lax.broadcasted_iota(jnp.int32, shape, dim)

    def flat(left, right):
        return lax.dot_general(left, right, (((1,), (1,)), ((), ())), preferred_element_type=f32)

    ids = ids_ref[n]
    digit = iota((128, width), 0)
    high = (digit == ids // 128).astype(bf)
    low = (digit == ids % 128).astype(bf)
    prior = jnp.sum(low.astype(f32) * jnp.dot(counts[...].astype(bf), high, preferred_element_type=f32), axis=0, keepdims=True)
    across = jnp.broadcast_to(ids.astype(f32), (width, width))
    same = jnp.where((across == across.T) & (iota((width, width), 0) < iota((width, width), 1)), 1.0, 0.0)
    again = jnp.where(prior + jnp.sum(same, axis=0, keepdims=True) > 0, 1.0, 0.0)
    counts[...] = counts[...] + flat(low, high)
    lane = iota((1, width), 1)
    block = ((lane // LANES) * NODES + n).astype(f32)
    inner = (lane % LANES).astype(f32)
    once = 1.0 - again
    low_f = low.astype(f32)
    firsts[...] = firsts[...] + flat(
        jnp.concatenate([low_f * (once * block), low_f * (once * inner)]).astype(bf), high
    )
    found = jnp.dot(firsts[...].astype(bf), high, preferred_element_type=f32)
    rep_block = jnp.sum(found[0:128] * low_f, axis=0, keepdims=True)
    rep_inner = jnp.sum(found[128:256] * low_f, axis=0, keepdims=True)
    before = jnp.dot(
        jnp.broadcast_to(again, (8, width)).astype(bf),
        jnp.where(iota((width, width), 0) < iota((width, width), 1), 1.0, 0.0).astype(bf),
        preferred_element_type=f32,
    )[0:1]
    slot = (before + used[0:1, 0:1]).astype(jnp.int32)
    used[...] = used[...] + jnp.sum(again, axis=1, keepdims=True)
    slot_low = jnp.where(digit == slot % 128, again, 0.0)
    slot_high = (digit == slot // 128).astype(bf)
    left = jnp.concatenate([slot_low * v for v in (block, inner, rep_block, rep_inner)]).astype(bf)
    lists[...] = lists[...] + flat(left, slot_high)


def lists_start(state):
    for ref in state:
        ref[...] = jnp.zeros_like(ref)


def lists_end(rim_ref, state, place_ref, rep_ref, rim_at_ref):
    counts, firsts, lists, used = state
    bf, f32 = jnp.bfloat16, jnp.float32
    index = lax.broadcasted_iota(jnp.int32, (128, 128), 0) * 128 + lax.broadcasted_iota(jnp.int32, (128, 128), 1)
    for k, ref in enumerate((place_ref, rep_ref)):
        at = lists[256 * k : 256 * k + 128] * 128.0 + lists[256 * k + 128 : 256 * k + 256]
        ref[...] = jnp.where(index < EXTRA, at.T.astype(jnp.int32), POINTS)[0:LIST_ROWS]
    rim = rim_ref[...]
    digit = lax.broadcasted_iota(jnp.int32, (128, RIM_PAD), 0)
    high = (digit == rim // 128).astype(bf)
    low = (digit == rim % 128).astype(f32)
    found = jnp.dot(firsts[...].astype(bf), high, preferred_element_type=f32)
    rep_block = jnp.sum(found[0:128] * low, axis=0, keepdims=True)
    rep_inner = jnp.sum(found[128:256] * low, axis=0, keepdims=True)
    rim_at_ref[...] = (rep_block * 128.0 + rep_inner).astype(jnp.int32)


def lists_kernel(ids_ref, rim_ref, place_ref, rep_ref, rim_at_ref, *state):
    lists_start(state)

    def go(n, _):
        lists_block(n, ids_ref, state)
        return 0
    lax.fori_loop(0, NODES, go, 0)
    lists_end(rim_ref, state, place_ref, rep_ref, rim_at_ref)


LIST_STATE = [
    pltpu.VMEM((128, 128), jnp.float32),
    pltpu.VMEM((256, 128), jnp.float32),
    pltpu.VMEM((512, 128), jnp.float32),
    pltpu.VMEM((8, 128), jnp.float32),
]
LIST_SHAPES = (
    jax.ShapeDtypeStruct((LIST_ROWS, 128), jnp.int32),
    jax.ShapeDtypeStruct((LIST_ROWS, 128), jnp.int32),
    jax.ShapeDtypeStruct((1, RIM_PAD), jnp.int32),
)


def node_lists(connect, edges):
    vmem = pl.BlockSpec(memory_space=pltpu.VMEM)
    rim = jnp.pad(edges.reshape(1, -1), ((0, 0), (0, RIM_PAD - 2 * RIM)))
    return pl.pallas_call(
        lists_kernel,
        out_shape=LIST_SHAPES,
        in_specs=[vmem] * 2,
        out_specs=(vmem,) * 3,
        scratch_shapes=LIST_STATE,
        compiler_params=pltpu.CompilerParams(vmem_limit_bytes=VMEM_LIMIT),
        name="lists",
    )(connect.reshape(NODES, 1, E_DEV), rim)


def gather_kernel(place_ref, rep_ref, rim_ref, table_ref, summed_ref, rims_ref, table, sems):
    load = pltpu.make_async_copy(table_ref, table.at[pl.ds(0, POINTS)], sems.at[0])
    load.start()
    table[pl.ds(POINTS, 8)] = jnp.zeros((8, 128), jnp.float32)
    load.wait()

    def add(t, _):
        for k in range(8):
            at = pl.ds(rep_ref[t // 16, (t % 16) * 8 + k], 1)
            table[at] = table[at] + table[pl.ds(place_ref[t // 16, (t % 16) * 8 + k], 1)]
        return 0
    lax.fori_loop(0, (EXTRA + 7) // 8, add, 0)
    store = pltpu.make_async_copy(table.at[pl.ds(0, POINTS)], summed_ref, sems.at[0])
    store.start()

    def pick(t, _):
        for k in range(9):
            rims_ref[pl.ds(t * 9 + k, 1)] = table[pl.ds(rim_ref[0, t * 9 + k], 1)]
        return 0
    lax.fori_loop(0, 2 * RIM // 9, pick, 0)
    store.wait()


def spread_kernel(place_ref, rep_ref, rim_ref, summed_ref, lower_ref, upper_ref, out_ref, table, sems):
    load = pltpu.make_async_copy(summed_ref, table.at[pl.ds(0, POINTS)], sems.at[0])
    load.start()
    table[pl.ds(POINTS, 8)] = jnp.zeros((8, 128), jnp.float32)
    load.wait()

    def add(t, _):
        for k in range(9):
            at = pl.ds(rim_ref[0, t * 9 + k], 1)
            table[at] = table[at] + lower_ref[pl.ds(t * 9 + k, 1)]
        for k in range(9):
            at = pl.ds(rim_ref[0, RIM + t * 9 + k], 1)
            table[at] = table[at] + upper_ref[pl.ds(t * 9 + k, 1)]
        return 0
    lax.fori_loop(0, RIM // 9, add, 0)

    def spread(t, _):
        vals = [table[pl.ds(rep_ref[t // 16, (t % 16) * 8 + k], 1)] for k in range(8)]
        for k in range(8):
            table[pl.ds(place_ref[t // 16, (t % 16) * 8 + k], 1)] = vals[k]
        return 0
    lax.fori_loop(0, (EXTRA + 7) // 8, spread, 0)

    def write(t, _):
        h, i = t // 8, t % 8
        parts = []
        for j in range(8):
            begin = pl.multiple_of((h * NODES + i * 8 + j) * LANES, LANES)
            cols = table[pl.ds(begin, LANES)].T
            parts.append(cols[0:48] / cols[48:49])
        block = jnp.swapaxes(jnp.stack(parts), 0, 1)
        out_ref[:, pl.ds(pl.multiple_of(i * 8, 8), 8), pl.ds(pl.multiple_of(h * LANES, LANES), LANES)] = block
        return 0
    lax.fori_loop(0, 16, write, 0)


def assemble(table, connect, edges):
    place, rep, rim_at = node_lists(connect, edges)
    smem = pl.BlockSpec(memory_space=pltpu.SMEM)
    vmem = pl.BlockSpec(memory_space=pltpu.VMEM)
    hbm = pl.BlockSpec(memory_space=pl.ANY)
    f32 = jnp.float32
    params = pltpu.CompilerParams(vmem_limit_bytes=VMEM_LIMIT)
    scratch = [pltpu.VMEM((POINTS + 8, 128), f32), pltpu.SemaphoreType.DMA((1,))]
    summed, rims = pl.pallas_call(
        gather_kernel,
        out_shape=(jax.ShapeDtypeStruct((POINTS, 128), f32), jax.ShapeDtypeStruct((2 * RIM, 128), f32)),
        in_specs=[smem, smem, smem, hbm],
        out_specs=(hbm, vmem),
        scratch_shapes=scratch,
        compiler_params=params,
        name="gather",
    )(place, rep, rim_at, table.reshape(POINTS, 128))
    count = lax.axis_size("mesh")
    up = [(i, (i + 1) % count) for i in range(count)]
    down = [(j, i) for i, j in up]
    from_lower = lax.ppermute(rims[RIM:], "mesh", up)
    from_upper = lax.ppermute(rims[:RIM], "mesh", down)
    return pl.pallas_call(
        spread_kernel,
        out_shape=jax.ShapeDtypeStruct((3 * COEFS, NODES, E_DEV), f32),
        in_specs=[smem, smem, smem, hbm, vmem, vmem],
        out_specs=vmem,
        scratch_shapes=scratch,
        compiler_params=params,
        name="spread",
    )(place, rep, rim_at, summed, from_lower, from_upper)


def body(adj_modes, base_flow, geometry, mass, connect, edge_nodes):
    me = lax.axis_index("four")
    geo = lax.dynamic_slice_in_dim(geometry, me * 4, 4, 1).reshape(4, 4, 1, E_DEV)
    table = step(adj_modes, base_flow, geo, mass.reshape(NODES, 1, E_DEV))
    out = assemble(table, connect, edge_nodes[0])
    return out.reshape(adj_modes.shape)


def solution(mesh):
    return jax.shard_map(
        body,
        mesh=mesh,
        in_specs=(
            P(None, "four", None, "mesh"),
            P(None, None, "four", "mesh"),
            P(None, None, "mesh"),
            P(None, "mesh"),
            P(None, "mesh"),
            P("mesh", None, None),
        ),
        out_specs=P(None, "four", None, "mesh"),
        check_vma=False,
    )
```

```python
import functools
import math

import jax
import jax.numpy as jnp
import numpy as np
from jax import lax
from jax.experimental import pallas as pl
from jax.experimental.pallas import tpu as pltpu
from jax.sharding import PartitionSpec as P

NP = 8
NODES = 64
PLANES = 256
UNIQUE = 12825
E_DEV = 256
POINTS = NODES * E_DEV
EXTRA = POINTS - UNIQUE
BATCH = 8
LISTED = (EXTRA + BATCH + 127) // 128 * 128
LIST_ROWS = (LISTED // 128 + 8) // 8 * 8
RIM = 225
RIM_PAD = 256
HALVES = 2
LANES = E_DEV // HALVES
N_MESH = 16
GROUP = 16
COEFS = PLANES // GROUP
STEP_SIZE = 0.1
HIGH = lax.Precision.HIGHEST
MESH = pl.DeviceIdType.MESH
VMEM_LIMIT = 60 * 2**20


def legendre_values(degree, point):
    before = 1.0
    current = point
    for order in range(1, degree):
        after = ((2 * order + 1) * point * current - order * before) / (order + 1)
        before = current
        current = after
    return (current, before)


def gll_derivative(points_n):
    degree = points_n - 1
    points = []
    for index in range(points_n):
        point = -math.cos(math.pi * index / degree)
        for sweep in range(100):
            top_val, below_val = legendre_values(degree, point)
            point = point - (point * top_val - below_val) / (points_n * top_val)
        points.append(point)
    values = [legendre_values(degree, point)[0] for point in points]
    rows = [
        [
            0.0 if r == c else values[r] / (values[c] * (points[r] - points[c]))
            for c in range(points_n)
        ]
        for r in range(points_n)
    ]
    rows[0][0] = -degree * (degree + 1) / 4.0
    rows[degree][degree] = degree * (degree + 1) / 4.0
    return np.asarray(rows, np.float32)


def plane_tables():
    plane = np.arange(PLANES)
    wave = plane // 2
    phase = (plane[:, None] * wave[None, :] % PLANES) * (2.0 * math.pi / PLANES)
    synth = np.where(plane[None, :] % 2 == 1, np.sin(phase), np.cos(phase))
    synth[:, 1] = 1 - 2 * (plane % 2)
    scales = np.where(wave == 0, 1.0 / PLANES, 2.0 / PLANES)
    analysis = synth.T * scales[:, None]
    number = wave * (2.0 / PLANES)
    axial = np.zeros((PLANES, PLANES))
    axial[plane[::2], plane[1::2]] = number[::2]
    axial[plane[1::2], plane[::2]] = -number[1::2]
    both = np.concatenate([synth, synth @ axial])
    return both.astype(np.float32), (STEP_SIZE * analysis).astype(np.float32)


def step_kernel(
    u_ref, base_ref, geometry_ref, mass_ref, ids_ref, rim_ref, synth_ref, anal_ref,
    table_ref, place_ref, rep_ref, rim_at_ref, rims_ref,
    ut, along, rows, slopes, base, stage, inputs, fields, forcing, back, returned, table,
    row_send, relay_send, slope_send, back_send, row_recv, slope_recv, back_recv,
    own_sem, stage_sem, table_sem, geo, rim_ids, rims, met, rim_send, rim_recv, *lists_state,
):
    deriv = gll_derivative(NP)
    me = lax.axis_index("four")
    x, z = me // 8, me % 8
    odd = z % 2
    sign = 1 - 2 * odd
    partner = x * 8 + z + sign

    def remote(src, dst, send, recv, to):
        return pltpu.make_async_remote_copy(
            src_ref=src, dst_ref=dst, send_sem=send, recv_sem=recv,
            device_id={"four": to}, device_id_type=MESH,
        )

    def source(dx, k):
        return ((x + dx) % 2) * 8 + (z - sign * k + 8) % 8

    def target(dx, k):
        off = (0, 2, -1, -3)[k]
        return ((x + dx) % 2) * 8 + (z + sign * off + 8) % 8

    def pair(dev):
        return pl.multiple_of((dev // 2) * 8, 8)

    def stage_copy(f):
        return pltpu.make_async_copy(base_ref.at[f], stage.at[f % 2], stage_sem.at[f % 2])

    def turn(h):
        def block(t, _):
            c = t // 8
            i = pl.multiple_of((t % 8) * 8, 8)
            ut[h, c, pl.ds(i, 8)] = jnp.swapaxes(u_ref[c, :, pl.ds(i, 8), pl.ds(h * LANES, LANES)], 0, 1)
            return 0
        lax.fori_loop(0, 24, block, 0)

    def differentiate(h):
        def block(t, _):
            c, j = t // 8, t % 8
            vals = [ut[h, c, 8 * i + j] for i in range(8)]
            for i in range(8):
                total = vals[0] * float(deriv[i, 0])
                for k in range(1, 8):
                    total = total + vals[k] * float(deriv[i, k])
                along[h, c, 8 * i + j] = total
            return 0
        lax.fori_loop(0, 24, block, 0)

    def row_copy(h, dx, k):
        to = target(dx, k)
        return remote(ut.at[h, :, pl.ds(pair(to), 8)], rows.at[h, me], row_send.at[h, dx * 4 + k], row_recv.at[h, me], to)

    def own_relay(h):
        return remote(ut.at[h, :, pl.ds(pair(me), 8)], rows.at[h, me], relay_send.at[h, 0], row_recv.at[h, me], partner)

    def relay(h, dx, k):
        src = source(dx, k)
        return remote(rows.at[h, src], rows.at[h, src], relay_send.at[h, dx * 4 + k], row_recv.at[h, src], partner)

    def far_source(dx, k):
        return ((x + dx) % 2) * 8 + (z + sign + sign * k + 8) % 8

    def row_wait(h, src):
        remote(rows.at[h, src], rows.at[h, src], relay_send.at[h, 0], row_recv.at[h, src], partner).wait_recv()

    def slope_copy(h, t):
        to = (me + t) % GROUP
        return remote(
            along.at[h, :, pl.ds(to * 4, 4)], slopes.at[h, me], slope_send.at[h, t], slope_recv.at[h, me], to
        )

    def slope_wait(h, t):
        src = (me + t) % GROUP
        remote(slopes.at[h, src], slopes.at[h, src], slope_send.at[h, t], slope_recv.at[h, src], src).wait_recv()

    def back_copy(h, t):
        to = (me + t) % GROUP
        return remote(back.at[h, to], returned.at[h, me], back_send.at[h, t], back_recv.at[h, me], to)

    def back_wait(h, src):
        remote(returned.at[h, src], returned.at[h, src], back_send.at[h, 0], back_recv.at[h, src], partner).wait_recv()

    def own_copies(h):
        return (
            pltpu.make_async_copy(ut.at[h, :, pl.ds(pair(me), 8)], rows.at[h, me], own_sem.at[h, 0]),
            pltpu.make_async_copy(along.at[h, :, pl.ds(me * 4, 4)], slopes.at[h, me], own_sem.at[h, 1]),
        )

    def own_back(h):
        return pltpu.make_async_copy(back.at[h, me], returned.at[h, me], own_sem.at[h, 2])

    NEAR = [(1, 0), (0, 1), (1, 1), (0, 2), (1, 2), (0, 3), (1, 3)]
    SENT = [(0, 3), (1, 3), (0, 1), (1, 1), (0, 2), (1, 2), (1, 0)]

    def each(fn):
        def go(t, _):
            fn(t)
            return 0
        lax.fori_loop(1, GROUP, go, 0)

    def send_rows(h):
        for dx, k in SENT:
            row_copy(h, dx, k).start()
        own_relay(h).start()

    def send_slopes(h):
        each(lambda t: slope_copy(h, t).start())

    def relays(h):
        for dx, k in NEAR:
            row_wait(h, source(dx, k))
            relay(h, dx, k).start()

    def compute(h):
        for copy in own_copies(h):
            copy.wait()
        for k in range(4):
            for dx in range(2):
                row_wait(h, far_source(dx, k))
        each(lambda t: slope_wait(h, t))

        def gather(s, _):
            at = pl.ds(pl.multiple_of(s * COEFS, COEFS), COEFS)
            for c in range(3):
                line = [rows[h, s, c, j] for j in range(8)]
                for n in range(4):
                    total = None
                    for k in range(8):
                        term = line[k] * jnp.where(odd == 1, float(deriv[4 + n, k]), float(deriv[n, k]))
                        total = term if total is None else total + term
                    inputs[n, at, pl.ds(c * LANES, LANES)] = jnp.where(odd == 1, line[4 + n], line[n])
                    inputs[n, at, pl.ds((3 + c) * LANES, LANES)] = total
                    inputs[n, at, pl.ds((6 + c) * LANES, LANES)] = slopes[h, s, c, n]
            return 0
        lax.fori_loop(0, GROUP, gather, 0)

        def node(n, _):
            fields[:, 0 : 9 * LANES] = jnp.dot(
                synth_ref[0:PLANES], inputs[n], precision=HIGH, preferred_element_type=jnp.float32
            )
            fields[:, 9 * LANES : 12 * LANES] = jnp.dot(
                synth_ref[PLANES : 2 * PLANES], inputs[n, :, 0 : 3 * LANES],
                precision=HIGH, preferred_element_type=jnp.float32,
            )
            metric = [geo[g, n, :, pl.ds(h * LANES, LANES)] for g in range(4)]

            def planes(p, _):
                at = pl.ds(pl.multiple_of(p * 16, 16), 16)
                flow = [base[f, n, at, pl.ds(h * LANES, LANES)].astype(jnp.float32) for f in range(12)]
                get = lambda f: fields[at, f * LANES : (f + 1) * LANES]
                on_r = flow[0] * metric[0] + flow[1] * metric[2]
                on_s = flow[0] * metric[1] + flow[1] * metric[3]
                vel = [get(c) for c in range(3)]
                for c in range(3):
                    total = vel[0] * flow[3 + 3 * c] + vel[1] * flow[4 + 3 * c] + vel[2] * flow[5 + 3 * c]
                    total = total - on_r * get(6 + c) - on_s * get(3 + c) - flow[2] * get(9 + c)
                    forcing[at, c * LANES : (c + 1) * LANES] = total
                return 0
            lax.fori_loop(0, PLANES // 16, planes, 0)
            modes = jnp.dot(anal_ref[...], forcing[...], precision=HIGH, preferred_element_type=jnp.float32)
            for c in range(3):
                back[h, :, c, n] = modes[:, c * LANES : (c + 1) * LANES].reshape(GROUP, COEFS, LANES)
            return 0
        lax.fori_loop(0, 4, node, 0)

    def table_copy(h, s):
        at = pl.ds(pl.multiple_of((h * NODES + 4 * s) * LANES, 4 * LANES), 4 * LANES)
        return pltpu.make_async_copy(table.at[at], table_ref.at[at], table_sem.at[h, s])

    def four_rows(block, s):
        return jnp.where(s % 2 == 1, block[4:8], block[0:4])

    def rim_start():
        for k in range(2):
            row = jnp.concatenate([rim_ref[0, k : k + 1], jnp.full((1, RIM_PAD - RIM), -1, jnp.int32)], axis=1)
            rim_ids[k * RIM_PAD : (k + 1) * RIM_PAD] = jnp.broadcast_to(row.astype(jnp.float32), (128, RIM_PAD)).T
        rims[...] = jnp.zeros_like(rims)

    def rim_sums(h, s, ids):
        at = pl.ds(pl.multiple_of((h * NODES + 4 * s) * LANES, 4 * LANES), 4 * LANES)
        rest = table[at, 0:LANES]
        pieces = []
        for _ in range(3):
            pieces.append(rest.astype(jnp.bfloat16))
            rest = rest - pieces[-1].astype(jnp.float32)
        hit = jnp.concatenate(
            [(rim_ids[...] == ids[n : n + 1].astype(jnp.float32)).astype(jnp.bfloat16) for n in range(4)], axis=1
        )
        sums = jnp.dot(hit, jnp.concatenate(pieces, axis=1), preferred_element_type=jnp.float32)
        rims[...] = rims[...] + (sums[:, 0:128] + (sums[:, 128:256] + sums[:, 256:384]))

    def rim_copy(side):
        to = (lax.axis_index("mesh") + (N_MESH - 1 if side == 0 else 1)) % N_MESH
        return pltpu.make_async_remote_copy(
            src_ref=rims.at[pl.ds(side * RIM_PAD, RIM_PAD)], dst_ref=met.at[pl.ds((1 - side) * RIM_PAD, RIM_PAD)],
            send_sem=rim_send.at[side], recv_sem=rim_recv.at[1 - side],
            device_id={"mesh": to}, device_id_type=MESH,
        )

    def finish(h, s):
        tile = pl.ds(pl.multiple_of((s // 2) * 8, 8), 8)
        weights = four_rows(mass_ref[tile, pl.ds(h * LANES, LANES)], s)
        for n in range(4):
            at = 4 * s + n
            weight = weights[n : n + 1]
            parts = [(ut[h, c, at] + returned[h, s, c, n]) * weight for c in range(3)]
            parts.append(jnp.broadcast_to(weight, (8, LANES)))
            parts.append(jnp.zeros((128 - 56, LANES), jnp.float32))
            begin = pl.multiple_of((h * NODES + at) * LANES, LANES)
            table[pl.ds(begin, LANES)] = jnp.concatenate(parts).T
        table_copy(h, s).start()
        rim_sums(h, s, four_rows(ids_ref[tile, pl.ds(h * LANES, LANES)], s))

    def lists_part(first, last):
        def go(i, _):
            lists_block(i, ids_ref, lists_state)
            return 0
        lax.fori_loop(first, last, go, 0)

    stage_copy(0).start()
    stage_copy(1).start()
    barrier = pltpu.get_barrier_semaphore()
    each(lambda t: pl.semaphore_signal(barrier, inc=1, device_id={"four": (me + t) % GROUP}, device_id_type=MESH))
    for off in (1, N_MESH - 1):
        pl.semaphore_signal(
            barrier, inc=1, device_id={"mesh": (lax.axis_index("mesh") + off) % N_MESH}, device_id_type=MESH
        )
    turn(0)
    pl.semaphore_wait(barrier, GROUP + 1)
    send_rows(0)
    differentiate(0)
    send_slopes(0)
    for copy in own_copies(0):
        copy.start()
    turn(1)
    differentiate(1)
    for copy in own_copies(1):
        copy.start()

    for f in range(12):
        stage_copy(f).wait()

        def move(t, _):
            p = pl.multiple_of(t * 64, 64)
            block = stage[f % 2, pl.ds(p, 64)].astype(jnp.float32)
            base[f, :, pl.ds(p, 64), :] = jnp.swapaxes(block, 0, 1).astype(jnp.bfloat16)
            return 0
        lax.fori_loop(0, 4, move, 0)
        if f + 2 < 12:
            stage_copy(f + 2).start()

    for g in range(4):
        own = four_rows(geometry_ref[g, pl.ds(pair(me), 8), :], me)
        for n in range(4):
            geo[g, n] = own[n : n + 1]

    relays(0)
    send_rows(1)
    send_slopes(1)
    lists_start(lists_state)
    rim_start()
    lists_part(0, 4)
    compute(0)
    own_back(0).start()
    relays(1)
    each(lambda t: back_copy(0, t).start())
    lists_part(4, 8)
    lists_end(rim_ref, lists_state, place_ref, rep_ref, rim_at_ref)
    compute(1)
    own_back(1).start()
    each(lambda t: back_copy(1, t).start())

    for h in range(HALVES):
        own_back(h).wait()
        finish(h, me)

        def arrive(t, _):
            src = (me + t) % GROUP
            back_wait(h, src)
            finish(h, src)
            return 0
        lax.fori_loop(1, GROUP, arrive, 0)

    for side in range(2):
        rim_copy(side).start()
    for side in range(2):
        rim_copy(side).wait_recv()
        rim_copy(side).wait_send()
    rims_ref[...] = rims[...] + met[...]

    for h in range(HALVES):
        for dx, k in SENT:
            row_copy(h, dx, k).wait_send()
        own_relay(h).wait_send()
        for dx, k in NEAR:
            relay(h, dx, k).wait_send()
        each(lambda t: slope_copy(h, t).wait_send())
        each(lambda t: back_copy(h, t).wait_send())

        def drained(s, _):
            table_copy(h, s).wait()
            return 0
        lax.fori_loop(0, GROUP, drained, 0)


def step(u, base, geometry, mass, ids, rim):
    synth, anal = plane_tables()
    vmem = pl.BlockSpec(memory_space=pltpu.VMEM)
    hbm = pl.BlockSpec(memory_space=pl.ANY)
    f32 = jnp.float32
    dma = pltpu.SemaphoreType.DMA
    return pl.pallas_call(
        step_kernel,
        out_shape=(
            jax.ShapeDtypeStruct((POINTS, 128), f32),
            jax.ShapeDtypeStruct((LIST_ROWS, 128), jnp.int32),
            jax.ShapeDtypeStruct((LIST_ROWS, 128), jnp.int32),
            jax.ShapeDtypeStruct((2, RIM_PAD), jnp.int32),
            jax.ShapeDtypeStruct((2 * RIM_PAD, 128), f32),
        ),
        in_specs=[vmem, hbm] + [vmem] * 6,
        out_specs=(hbm, vmem, vmem, vmem, vmem),
        scratch_shapes=[
            pltpu.VMEM((HALVES, 3, NODES, COEFS, LANES), f32),
            pltpu.VMEM((HALVES, 3, NODES, COEFS, LANES), f32),
            pltpu.VMEM((HALVES, GROUP, 3, 8, COEFS, LANES), f32),
            pltpu.VMEM((HALVES, GROUP, 3, 4, COEFS, LANES), f32),
            pltpu.VMEM((12, 4, PLANES, E_DEV), jnp.bfloat16),
            pltpu.VMEM((2, PLANES, 4, E_DEV), jnp.bfloat16),
            pltpu.VMEM((4, PLANES, 9 * LANES), f32),
            pltpu.VMEM((PLANES, 12 * LANES), f32),
            pltpu.VMEM((PLANES, 3 * LANES), f32),
            pltpu.VMEM((HALVES, GROUP, 3, 4, COEFS, LANES), f32),
            pltpu.VMEM((HALVES, GROUP, 3, 4, COEFS, LANES), f32),
            pltpu.VMEM((POINTS, 128), f32),
            dma((HALVES, 8)), dma((HALVES, 8)), dma((HALVES, GROUP)), dma((HALVES, GROUP)),
            dma((HALVES, GROUP)), dma((HALVES, GROUP)), dma((HALVES, GROUP)),
            dma((HALVES, 3)), dma((2,)), dma((HALVES, GROUP)),
            pltpu.VMEM((4, 4, 1, E_DEV), f32),
            pltpu.VMEM((2 * RIM_PAD, 128), f32),
            pltpu.VMEM((2 * RIM_PAD, 128), f32),
            pltpu.VMEM((2 * RIM_PAD, 128), f32),
            dma((2,)), dma((2,)),
            pltpu.VMEM((128, 128), f32),
            pltpu.VMEM((256, 128), f32),
            pltpu.VMEM((512, 128), f32),
            pltpu.VMEM((8, 128), f32),
        ],
        compiler_params=pltpu.CompilerParams(
            collective_id=0, has_side_effects=True, vmem_limit_bytes=VMEM_LIMIT
        ),
        name="step",
    )(u, base, geometry, mass, ids, rim, jnp.asarray(synth), jnp.asarray(anal))


def lists_block(i, ids_ref, state):
    tile = ids_ref[pl.ds(pl.multiple_of(i * 8, 8), 8), :]
    for j in range(8):
        lists_row(i * 8 + j, tile[j : j + 1], state)


def lists_row(n, ids, state):
    counts, firsts, lists, used = state
    bf, f32 = jnp.bfloat16, jnp.float32
    width = E_DEV

    def iota(shape, dim):
        return lax.broadcasted_iota(jnp.int32, shape, dim)

    def flat(left, right):
        return lax.dot_general(left, right, (((1,), (1,)), ((), ())), preferred_element_type=f32)

    digit = iota((128, width), 0)
    high = (digit == ids // 128).astype(bf)
    low = (digit == ids % 128).astype(bf)
    low_f = low.astype(f32)
    earlier = iota((width, width), 0) < iota((width, width), 1)
    prior = jnp.sum(low_f * jnp.dot(counts[...].astype(bf), high, preferred_element_type=f32), axis=0, keepdims=True)
    across = jnp.broadcast_to(ids.astype(f32), (width, width))
    same = jnp.where((across == across.T) & earlier, 1.0, 0.0)
    prior = prior + jnp.sum(same, axis=0, keepdims=True)
    counts[...] = counts[...] + flat(low, high)
    lane = iota((1, width), 1)
    block = ((lane // LANES) * NODES + n).astype(f32)
    inner = (lane % LANES).astype(f32)
    once = jnp.where(prior == 0, 1.0, 0.0)
    firsts[...] = firsts[...] + flat(
        jnp.concatenate([low_f * (once * block), low_f * (once * inner)]).astype(bf), high
    )
    found = jnp.dot(firsts[...].astype(bf), high, preferred_element_type=f32)
    rep_block = jnp.sum(found[0:128] * low_f, axis=0, keepdims=True)
    rep_inner = jnp.sum(found[128:256] * low_f, axis=0, keepdims=True)
    second = jnp.where(prior == 1, 1.0, 0.0)
    further = jnp.where(prior > 1, 1.0, 0.0)
    kinds = jnp.concatenate([second, further, jnp.zeros((6, width), f32)])
    before = jnp.dot(
        kinds.astype(bf), jnp.where(earlier, 1.0, 0.0).astype(bf), preferred_element_type=f32
    ) + used[:, 0:1]
    used[...] = used[...] + jnp.sum(kinds, axis=1, keepdims=True)
    slot = jnp.where(second > 0, before[0:1], LISTED - 1 - before[1:2]).astype(jnp.int32)
    slot_low = jnp.where(digit == slot % 128, second + further, 0.0)
    slot_high = (digit == slot // 128).astype(bf)
    left = jnp.concatenate([slot_low * v for v in (block, inner, rep_block, rep_inner)]).astype(bf)
    lists[...] = lists[...] + flat(left, slot_high)


def lists_start(state):
    for ref in state:
        ref[...] = jnp.zeros_like(ref)


def lists_end(rim_ref, state, place_ref, rep_ref, rim_at_ref):
    counts, firsts, lists, used = state
    bf, f32 = jnp.bfloat16, jnp.float32
    index = lax.broadcasted_iota(jnp.int32, (128, 128), 0) * 128 + lax.broadcasted_iota(jnp.int32, (128, 128), 1)
    front = used[0:1, 0:1].astype(jnp.int32)
    end = LISTED - used[1:2, 0:1].astype(jnp.int32)
    for k, ref in enumerate((place_ref, rep_ref)):
        at = lists[256 * k : 256 * k + 128] * 128.0 + lists[256 * k + 128 : 256 * k + 256]
        filled = (index < front) | (index >= end)
        entries = jnp.where(filled, at.T.astype(jnp.int32), POINTS)
        ref[...] = jnp.where(index < LISTED, entries, front)[0:LIST_ROWS]
    rim = rim_ref[0]
    rim_at_ref[...] = jnp.zeros_like(rim_at_ref)
    digit = lax.broadcasted_iota(jnp.int32, (128, RIM), 0)
    for k in range(2):
        ids = rim[k : k + 1]
        high = (digit == ids // 128).astype(bf)
        low = (digit == ids % 128).astype(f32)
        found = jnp.dot(firsts[...].astype(bf), high, preferred_element_type=f32)
        rep_block = jnp.sum(found[0:128] * low, axis=0, keepdims=True)
        rep_inner = jnp.sum(found[128:256] * low, axis=0, keepdims=True)
        rim_at_ref[k : k + 1, 0:RIM] = (rep_block * 128.0 + rep_inner).astype(jnp.int32)


def assemble_kernel(place_ref, rep_ref, rim_ref, table_ref, rims_ref, out_ref, table, out, sem, out_sem):
    load = pltpu.make_async_copy(table_ref, table.at[pl.ds(0, POINTS)], sem.at[0])
    load.start()
    table[pl.ds(POINTS, 8)] = jnp.zeros((8, 1, 128), jnp.float32)
    load.wait()
    front = place_ref[LIST_ROWS * 128 - 1]

    def add(t, _):
        at = [rep_ref[t * BATCH + k] for k in range(BATCH)]
        vals = [table[at[k]] + table[place_ref[t * BATCH + k]] for k in range(BATCH)]
        for k in range(BATCH):
            table[at[k]] = vals[k]
        return 0
    lax.fori_loop(0, (front + BATCH - 1) // BATCH, add, 0)

    def add_further(t, _):
        at = rep_ref[LISTED - 1 - t]
        table[at] = table[at] + table[place_ref[LISTED - 1 - t]]
        return 0
    lax.fori_loop(0, EXTRA - front, add_further, 0)

    def meet(t, _):
        for side in range(2):
            for k in range(9):
                table[rim_ref[side * RIM_PAD + t * 9 + k]] = rims_ref[side * RIM_PAD + t * 9 + k]
        return 0
    lax.fori_loop(0, RIM // 9, meet, 0)

    def spread(t, _):
        vals = [table[rep_ref[t * BATCH + k]] for k in range(BATCH)]
        for k in range(BATCH):
            table[place_ref[t * BATCH + k]] = vals[k]
        return 0
    lax.fori_loop(0, LISTED // BATCH, spread, 0)

    def block_copy(t):
        at = (
            slice(None),
            pl.ds(pl.multiple_of((t % 8) * 8, 8), 8),
            pl.ds(pl.multiple_of((t // 8) * LANES, LANES), LANES),
        )
        return pltpu.make_async_copy(out.at[at], out_ref.at[at], out_sem.at[t])

    def write(t, _):
        h, i = t // 8, t % 8
        parts = []
        for j in range(8):
            begin = pl.multiple_of((h * NODES + i * 8 + j) * LANES, LANES)
            cols = table[pl.ds(begin, LANES)].reshape(LANES, 128).T
            parts.append(cols[0:48] / cols[48:49])
        block = jnp.swapaxes(jnp.stack(parts), 0, 1)
        out[:, pl.ds(pl.multiple_of(i * 8, 8), 8), pl.ds(pl.multiple_of(h * LANES, LANES), LANES)] = block
        block_copy(t).start()
        return 0
    lax.fori_loop(0, 16, write, 0)

    def written(t, _):
        block_copy(t).wait()
        return 0
    lax.fori_loop(0, 16, written, 0)


def assemble(table, place, rep, rim_at, rims):
    smem = pl.BlockSpec(memory_space=pltpu.SMEM)
    vmem = pl.BlockSpec(memory_space=pltpu.VMEM)
    hbm = pl.BlockSpec(memory_space=pl.ANY)
    f32 = jnp.float32
    return pl.pallas_call(
        assemble_kernel,
        out_shape=jax.ShapeDtypeStruct((3 * COEFS, NODES, E_DEV), f32),
        in_specs=[smem, smem, smem, hbm, vmem],
        out_specs=hbm,
        scratch_shapes=[
            pltpu.VMEM((POINTS + 8, 1, 128), f32),
            pltpu.VMEM((3 * COEFS, NODES, E_DEV), f32),
            pltpu.SemaphoreType.DMA((1,)),
            pltpu.SemaphoreType.DMA((16,)),
        ],
        compiler_params=pltpu.CompilerParams(vmem_limit_bytes=VMEM_LIMIT),
        name="assemble",
    )(
        place.reshape(-1), rep.reshape(-1), rim_at.reshape(-1),
        table.reshape(POINTS, 1, 128), rims.reshape(2 * RIM_PAD, 1, 128),
    )


def body(adj_modes, base_flow, geometry, mass, connect, edge_nodes):
    table, *lists = step(adj_modes, base_flow, geometry, mass, connect, edge_nodes)
    return assemble(table, *lists).reshape(adj_modes.shape)


def solution(mesh):
    return jax.shard_map(
        body,
        mesh=mesh,
        in_specs=(
            P(None, "four", None, "mesh"),
            P(None, None, "four", "mesh"),
            P(None, None, "mesh"),
            P(None, "mesh"),
            P(None, "mesh"),
            P("mesh", None, None),
        ),
        out_specs=P(None, "four", None, "mesh"),
        check_vma=False,
    )
```

```python
import functools
import math

import jax
import jax.numpy as jnp
import numpy as np
from jax import lax
from jax.experimental import pallas as pl
from jax.experimental.pallas import tpu as pltpu
from jax.sharding import PartitionSpec as P

NP = 8
NODES = 64
PLANES = 256
UNIQUE = 12825
E_DEV = 256
POINTS = NODES * E_DEV
EXTRA = POINTS - UNIQUE
BATCH = 8
LISTED = (EXTRA + BATCH + 127) // 128 * 128
LIST_ROWS = (LISTED // 128 + 8) // 8 * 8
PLACES = LIST_ROWS * 128
RIM = 225
RIM_PAD = 256
HALVES = 2
LANES = E_DEV // HALVES
N_MESH = 16
GROUP = 16
COEFS = PLANES // GROUP
STEP_SIZE = 0.1
HIGH = lax.Precision.HIGHEST
MESH = pl.DeviceIdType.MESH
VMEM_LIMIT = 60 * 2**20


def legendre_values(degree, point):
    before = 1.0
    current = point
    for order in range(1, degree):
        after = ((2 * order + 1) * point * current - order * before) / (order + 1)
        before = current
        current = after
    return (current, before)


def gll_derivative(points_n):
    degree = points_n - 1
    points = []
    for index in range(points_n):
        point = -math.cos(math.pi * index / degree)
        for sweep in range(100):
            top_val, below_val = legendre_values(degree, point)
            point = point - (point * top_val - below_val) / (points_n * top_val)
        points.append(point)
    values = [legendre_values(degree, point)[0] for point in points]
    rows = [
        [
            0.0 if r == c else values[r] / (values[c] * (points[r] - points[c]))
            for c in range(points_n)
        ]
        for r in range(points_n)
    ]
    rows[0][0] = -degree * (degree + 1) / 4.0
    rows[degree][degree] = degree * (degree + 1) / 4.0
    return np.asarray(rows, np.float32)


def plane_tables():
    plane = np.arange(PLANES)
    wave = plane // 2
    phase = (plane[:, None] * wave[None, :] % PLANES) * (2.0 * math.pi / PLANES)
    synth = np.where(plane[None, :] % 2 == 1, np.sin(phase), np.cos(phase))
    synth[:, 1] = 1 - 2 * (plane % 2)
    scales = np.where(wave == 0, 1.0 / PLANES, 2.0 / PLANES)
    analysis = synth.T * scales[:, None]
    number = wave * (2.0 / PLANES)
    axial = np.zeros((PLANES, PLANES))
    axial[plane[::2], plane[1::2]] = number[::2]
    axial[plane[1::2], plane[::2]] = -number[1::2]
    both = np.concatenate([synth, synth @ axial])
    return both.astype(np.float32), (STEP_SIZE * analysis).astype(np.float32)


def step_kernel(
    u_ref, base_ref, geometry_ref, mass_ref, ids_ref, rim_ref, synth_ref, anal_ref,
    table_ref, lists_ref, rims_ref,
    u, ut, along, rows, slopes, base, stage, inputs, fields, forcing, back, returned, table,
    row_send, relay_send, slope_send, back_send, row_recv, slope_recv, back_recv,
    own_sem, stage_sem, table_sem, u_sem, geo, rim_ids, rim_parts, rims, met, rim_send, rim_recv, *lists_state,
):
    deriv = gll_derivative(NP)
    me = lax.axis_index("four")
    x, z = me // 8, me % 8
    odd = z % 2
    sign = 1 - 2 * odd
    partner = x * 8 + z + sign

    def remote(src, dst, send, recv, to):
        return pltpu.make_async_remote_copy(
            src_ref=src, dst_ref=dst, send_sem=send, recv_sem=recv,
            device_id={"four": to}, device_id_type=MESH,
        )

    def source(dx, k):
        return ((x + dx) % 2) * 8 + (z - sign * k + 8) % 8

    def target(dx, k):
        off = (0, 2, -1, -3)[k]
        return ((x + dx) % 2) * 8 + (z + sign * off + 8) % 8

    def pair(dev):
        return pl.multiple_of((dev // 2) * 8, 8)

    def stage_copy(f):
        return pltpu.make_async_copy(base_ref.at[f], stage.at[f % 2], stage_sem.at[f % 2])

    def u_copy(h):
        return pltpu.make_async_copy(u_ref.at[:, :, :, pl.ds(h * LANES, LANES)], u.at[h], u_sem.at[h])

    def turn(h):
        u_copy(h).wait()
        def block(t, _):
            c = t // 8
            i = pl.multiple_of((t % 8) * 8, 8)
            ut[h, c, pl.ds(i, 8)] = jnp.swapaxes(u[h, c, :, pl.ds(i, 8)], 0, 1)
            return 0
        lax.fori_loop(0, 24, block, 0)

    def differentiate(h):
        def block(t, _):
            c, j = t // 8, t % 8
            vals = [ut[h, c, 8 * i + j] for i in range(8)]
            for i in range(8):
                total = vals[0] * float(deriv[i, 0])
                for k in range(1, 8):
                    total = total + vals[k] * float(deriv[i, k])
                along[h, c, 8 * i + j] = total
            return 0
        lax.fori_loop(0, 24, block, 0)

    def u_rows(h, dev):
        return u_ref.at[:, :, pl.ds(pair(dev), 8), pl.ds(h * LANES, LANES)]

    def row_copy(h, dx, k):
        to = target(dx, k)
        return remote(u_rows(h, to), rows.at[h, me], row_send.at[h, dx * 4 + k], row_recv.at[h, me], to)

    def own_relay(h):
        return remote(u_rows(h, me), rows.at[h, me], relay_send.at[h, 0], row_recv.at[h, me], partner)

    def relay(h, dx, k):
        src = source(dx, k)
        return remote(rows.at[h, src], rows.at[h, src], relay_send.at[h, dx * 4 + k], row_recv.at[h, src], partner)

    def far_source(dx, k):
        return ((x + dx) % 2) * 8 + (z + sign + sign * k + 8) % 8

    def row_wait(h, src):
        remote(rows.at[h, src], rows.at[h, src], relay_send.at[h, 0], row_recv.at[h, src], partner).wait_recv()

    def slope_copy(h, t):
        to = (me + t) % GROUP
        return remote(
            along.at[h, :, pl.ds(to * 4, 4)], slopes.at[h, me], slope_send.at[h, t], slope_recv.at[h, me], to
        )

    def slope_wait(h, t):
        src = (me + t) % GROUP
        remote(slopes.at[h, src], slopes.at[h, src], slope_send.at[h, t], slope_recv.at[h, src], src).wait_recv()

    def back_copy(h, g, t):
        to = (me + t) % GROUP
        return remote(
            back.at[h, g, to], returned.at[h, g, me], back_send.at[h, g, t], back_recv.at[h, g, me], to
        )

    def back_wait(h, g, src):
        remote(
            returned.at[h, g, src], returned.at[h, g, src], back_send.at[h, g, 0], back_recv.at[h, g, src], partner
        ).wait_recv()

    def own_copies(h):
        return (
            pltpu.make_async_copy(u_rows(h, me), rows.at[h, me], own_sem.at[h, 0]),
            pltpu.make_async_copy(along.at[h, :, pl.ds(me * 4, 4)], slopes.at[h, me], own_sem.at[h, 1]),
        )

    def own_back(h, g):
        return pltpu.make_async_copy(back.at[h, g, me], returned.at[h, g, me], own_sem.at[h, 2 + g])

    def send_back(h, g):
        own_back(h, g).start()
        each(lambda t: back_copy(h, g, t).start())

    NEAR = [(1, 0), (0, 1), (1, 1), (0, 2), (1, 2), (0, 3), (1, 3)]
    SENT = [(0, 3), (1, 3), (0, 1), (1, 1), (0, 2), (1, 2), (1, 0)]

    def each(fn):
        def go(t, _):
            fn(t)
            return 0
        lax.fori_loop(1, GROUP, go, 0)

    def send_rows(h):
        for dx, k in SENT:
            row_copy(h, dx, k).start()
        own_relay(h).start()

    def send_slopes(h):
        each(lambda t: slope_copy(h, t).start())

    def relays(h):
        for dx, k in NEAR:
            row_wait(h, source(dx, k))
            relay(h, dx, k).start()

    def compute(h, after):
        for copy in own_copies(h):
            copy.wait()
        for k in range(4):
            for dx in range(2):
                row_wait(h, far_source(dx, k))
        each(lambda t: slope_wait(h, t))

        def gather(s, _):
            at = pl.ds(pl.multiple_of(s * COEFS, COEFS), COEFS)
            for c in range(3):
                turned = jnp.swapaxes(rows[h, s, c], 0, 1)
                line = [turned[j] for j in range(8)]
                for n in range(4):
                    total = None
                    for k in range(8):
                        term = line[k] * jnp.where(odd == 1, float(deriv[4 + n, k]), float(deriv[n, k]))
                        total = term if total is None else total + term
                    inputs[n, at, pl.ds(c * LANES, LANES)] = jnp.where(odd == 1, line[4 + n], line[n])
                    inputs[n, at, pl.ds((3 + c) * LANES, LANES)] = total
                    inputs[n, at, pl.ds((6 + c) * LANES, LANES)] = slopes[h, s, c, n]
            return 0
        lax.fori_loop(0, GROUP, gather, 0)

        def node(n, _):
            fields[:, 0 : 9 * LANES] = jnp.dot(
                synth_ref[0:PLANES], inputs[n], precision=HIGH, preferred_element_type=jnp.float32
            )
            fields[:, 9 * LANES : 12 * LANES] = jnp.dot(
                synth_ref[PLANES : 2 * PLANES], inputs[n, :, 0 : 3 * LANES],
                precision=HIGH, preferred_element_type=jnp.float32,
            )
            metric = [geo[g, n, :, pl.ds(h * LANES, LANES)] for g in range(4)]

            def planes(p, _):
                at = pl.ds(pl.multiple_of(p * 16, 16), 16)
                flow = [base[f, n, at, pl.ds(h * LANES, LANES)].astype(jnp.float32) for f in range(12)]
                get = lambda f: fields[at, f * LANES : (f + 1) * LANES]
                on_r = flow[0] * metric[0] + flow[1] * metric[2]
                on_s = flow[0] * metric[1] + flow[1] * metric[3]
                vel = [get(c) for c in range(3)]
                for c in range(3):
                    total = vel[0] * flow[3 + 3 * c] + vel[1] * flow[4 + 3 * c] + vel[2] * flow[5 + 3 * c]
                    total = total - on_r * get(6 + c) - on_s * get(3 + c) - flow[2] * get(9 + c)
                    forcing[at, c * LANES : (c + 1) * LANES] = total
                return 0
            lax.fori_loop(0, PLANES // 16, planes, 0)
            modes = jnp.dot(anal_ref[...], forcing[...], precision=HIGH, preferred_element_type=jnp.float32)
            for c in range(3):
                back[h, n // 2, :, n % 2, c] = modes[:, c * LANES : (c + 1) * LANES].reshape(GROUP, COEFS, LANES)
            return 0
        for g in range(2):
            lax.fori_loop(2 * g, 2 * g + 2, node, 0)
            after(g)

    def table_copy(h, g, s):
        at = pl.ds(pl.multiple_of((h * NODES + 4 * s + 2 * g) * LANES, 2 * LANES), 2 * LANES)
        return pltpu.make_async_copy(table.at[at], table_ref.at[at], table_sem.at[h, g, s])

    def four_rows(block, s):
        return jnp.where(s % 2 == 1, block[4:8], block[0:4])

    def rim_start():
        for k in range(2):
            row = jnp.concatenate([rim_ref[0, k : k + 1], jnp.full((1, RIM_PAD - RIM), -1, jnp.int32)], axis=1)
            rim_ids[k * RIM_PAD : (k + 1) * RIM_PAD] = jnp.broadcast_to(row.astype(jnp.float32), (128, RIM_PAD)).T
        rim_parts[...] = jnp.zeros_like(rim_parts)

    def rim_sums(values, ids):
        pieces = []
        for _ in range(3):
            pieces.append(values.astype(jnp.bfloat16))
            values = values - pieces[-1].astype(jnp.float32)
        hit = jnp.concatenate([(rim_ids[...] == row.astype(jnp.float32)).astype(jnp.bfloat16) for row in ids], axis=1)
        rim_parts[...] = rim_parts[...] + lax.dot_general(
            hit, jnp.concatenate(pieces), (((1,), (1,)), ((), ())), preferred_element_type=jnp.float32
        )

    def rim_total():
        parts = rim_parts[...]
        total = parts[:, 0:64] + (parts[:, 64:128] + parts[:, 128:192])
        rims[...] = jnp.concatenate([total, jnp.zeros_like(total)], axis=1)

    def rim_copy(side):
        to = (lax.axis_index("mesh") + (N_MESH - 1 if side == 0 else 1)) % N_MESH
        return pltpu.make_async_remote_copy(
            src_ref=rims.at[pl.ds(side * RIM_PAD, RIM_PAD)], dst_ref=met.at[pl.ds((1 - side) * RIM_PAD, RIM_PAD)],
            send_sem=rim_send.at[side], recv_sem=rim_recv.at[1 - side],
            device_id={"mesh": to}, device_id_type=MESH,
        )

    def finish(h, g, s):
        tile = pl.ds(pl.multiple_of((s // 2) * 8, 8), 8)
        half = pl.ds(h * LANES, LANES)
        weights = four_rows(mass_ref[tile, half], s)
        ids = four_rows(ids_ref[tile, half], s)
        tall = []
        for n in range(2):
            at = 4 * s + 2 * g + n
            weight = weights[2 * g + n : 2 * g + n + 1]
            parts = [(ut[h, c, at] + returned[h, g, s, n, c]) * weight for c in range(3)]
            parts.append(jnp.broadcast_to(weight, (8, LANES)))
            parts.append(jnp.zeros((8, LANES), jnp.float32))
            tall.append(jnp.concatenate(parts))
            begin = pl.multiple_of((h * NODES + at) * LANES, LANES)
            table[pl.ds(begin, LANES)] = jnp.concatenate([tall[-1], jnp.zeros((64, LANES), jnp.float32)]).T
        table_copy(h, g, s).start()
        rim_sums(jnp.concatenate(tall, axis=1), [ids[2 * g + n : 2 * g + n + 1] for n in range(2)])

    def lists_part(block):
        def go(i, _):
            block(i, ids_ref, lists_state)
            return 0
        lax.fori_loop(0, NODES // 8, go, 0)

    for h in range(HALVES):
        u_copy(h).start()
    barrier = pltpu.get_barrier_semaphore()
    each(lambda t: pl.semaphore_signal(barrier, inc=1, device_id={"four": (me + t) % GROUP}, device_id_type=MESH))
    for off in (1, N_MESH - 1):
        pl.semaphore_signal(
            barrier, inc=1, device_id={"mesh": (lax.axis_index("mesh") + off) % N_MESH}, device_id_type=MESH
        )
    pl.semaphore_wait(barrier, GROUP + 1)
    send_rows(0)
    turn(0)
    differentiate(0)
    send_slopes(0)
    for copy in own_copies(0):
        copy.start()
    stage_copy(0).start()
    stage_copy(1).start()
    turn(1)
    differentiate(1)
    for copy in own_copies(1):
        copy.start()

    for f in range(12):
        stage_copy(f).wait()

        def move(t, _):
            p = pl.multiple_of(t * 64, 64)
            block = stage[f % 2, pl.ds(p, 64)].astype(jnp.float32)
            base[f, :, pl.ds(p, 64), :] = jnp.swapaxes(block, 0, 1).astype(jnp.bfloat16)
            return 0
        lax.fori_loop(0, 4, move, 0)
        if f + 2 < 12:
            stage_copy(f + 2).start()

    for g in range(4):
        own = four_rows(geometry_ref[g, pl.ds(pair(me), 8), :], me)
        for n in range(4):
            geo[g, n] = own[n : n + 1]

    relays(0)
    send_rows(1)
    send_slopes(1)
    lists_start(rim_ref, lists_state)
    rim_start()
    lists_part(count_block)
    compute(0, lambda g: None)
    relays(1)
    for g in range(2):
        send_back(0, g)
    lists_part(list_block)
    lists_end(rim_ref, lists_state, lists_ref)
    compute(1, lambda g: send_back(1, g))

    for h in range(HALVES):
        for g in range(2):
            own_back(h, g).wait()
            finish(h, g, me)

            def arrive(t, _):
                src = (me + t) % GROUP
                back_wait(h, g, src)
                finish(h, g, src)
                return 0
            lax.fori_loop(1, GROUP, arrive, 0)
    rim_total()

    for side in range(2):
        rim_copy(side).start()
    for side in range(2):
        rim_copy(side).wait_recv()
        rim_copy(side).wait_send()
    rims_ref[...] = rims[...] + met[...]

    for h in range(HALVES):
        for dx, k in SENT:
            row_copy(h, dx, k).wait_send()
        own_relay(h).wait_send()
        for dx, k in NEAR:
            relay(h, dx, k).wait_send()
        each(lambda t: slope_copy(h, t).wait_send())
        for g in range(2):
            each(lambda t: back_copy(h, g, t).wait_send())

            def drained(s, _):
                table_copy(h, g, s).wait()
                return 0
            lax.fori_loop(0, GROUP, drained, 0)


def step(u, base, geometry, mass, ids, rim):
    synth, anal = plane_tables()
    vmem = pl.BlockSpec(memory_space=pltpu.VMEM)
    hbm = pl.BlockSpec(memory_space=pl.ANY)
    f32 = jnp.float32
    dma = pltpu.SemaphoreType.DMA
    return pl.pallas_call(
        step_kernel,
        out_shape=(
            jax.ShapeDtypeStruct((POINTS, 128), f32),
            jax.ShapeDtypeStruct((2 * LIST_ROWS + 8, 128), jnp.int32),
            jax.ShapeDtypeStruct((2 * RIM_PAD, 128), f32),
        ),
        in_specs=[hbm, hbm] + [vmem] * 6,
        out_specs=(hbm, vmem, vmem),
        scratch_shapes=[
            pltpu.VMEM((HALVES, 3, COEFS, NODES, LANES), f32),
            pltpu.VMEM((HALVES, 3, NODES, COEFS, LANES), f32),
            pltpu.VMEM((HALVES, 3, NODES, COEFS, LANES), f32),
            pltpu.VMEM((HALVES, GROUP, 3, COEFS, 8, LANES), f32),
            pltpu.VMEM((HALVES, GROUP, 3, 4, COEFS, LANES), f32),
            pltpu.VMEM((12, 4, PLANES, E_DEV), jnp.bfloat16),
            pltpu.VMEM((2, PLANES, 4, E_DEV), jnp.bfloat16),
            pltpu.VMEM((4, PLANES, 9 * LANES), f32),
            pltpu.VMEM((PLANES, 12 * LANES), f32),
            pltpu.VMEM((PLANES, 3 * LANES), f32),
            pltpu.VMEM((HALVES, 2, GROUP, 2, 3, COEFS, LANES), f32),
            pltpu.VMEM((HALVES, 2, GROUP, 2, 3, COEFS, LANES), f32),
            pltpu.VMEM((POINTS, 128), f32),
            dma((HALVES, 8)), dma((HALVES, 8)), dma((HALVES, GROUP)), dma((HALVES, 2, GROUP)),
            dma((HALVES, GROUP)), dma((HALVES, GROUP)), dma((HALVES, 2, GROUP)),
            dma((HALVES, 4)), dma((2,)), dma((HALVES, 2, GROUP)),
            dma((HALVES,)),
            pltpu.VMEM((4, 4, 1, E_DEV), f32),
            pltpu.VMEM((2 * RIM_PAD, 128), f32),
            pltpu.VMEM((2 * RIM_PAD, 192), f32),
            pltpu.VMEM((2 * RIM_PAD, 128), f32),
            pltpu.VMEM((2 * RIM_PAD, 128), f32),
            dma((2,)), dma((2,)),
            pltpu.VMEM((128, 128), f32),
            pltpu.VMEM((256, 128), f32),
            pltpu.VMEM((NODES, E_DEV), f32),
            pltpu.VMEM((128, 128), f32),
            pltpu.VMEM((512, 128), f32),
            pltpu.VMEM((8, 128), f32),
        ],
        compiler_params=pltpu.CompilerParams(
            collective_id=0, has_side_effects=True, vmem_limit_bytes=VMEM_LIMIT
        ),
        name="step",
    )(u, base, geometry, mass, ids, rim, jnp.asarray(synth), jnp.asarray(anal))


def iota(shape, dim):
    return lax.broadcasted_iota(jnp.int32, shape, dim)


def flat(left, right):
    return lax.dot_general(left, right, (((1,), (1,)), ((), ())), preferred_element_type=jnp.float32)


def digits(ids):
    digit = iota((128, ids.shape[1]), 0)
    return (digit == ids // 128).astype(jnp.bfloat16), (digit == ids % 128).astype(jnp.bfloat16)


def look_up(tables, high, low):
    found = jnp.dot(tables.astype(jnp.bfloat16), high, preferred_element_type=jnp.float32)
    return [
        jnp.sum(found[k : k + 128] * low, axis=0, keepdims=True) for k in range(0, tables.shape[0], 128)
    ]


def place_of(n):
    lane = iota((1, E_DEV), 1)
    return ((lane // LANES) * NODES + n).astype(jnp.float32), (lane % LANES).astype(jnp.float32)


def count_block(i, ids_ref, state):
    counts, firsts, priors = state[0], state[1], state[2]
    at = pl.ds(pl.multiple_of(i * 8, 8), 8)
    tile = ids_ref[at, :]
    kept = []
    for j in range(8):
        ids = tile[j : j + 1]
        high, low = digits(ids)
        low_f = low.astype(jnp.float32)
        across = jnp.broadcast_to(ids.astype(jnp.float32), (E_DEV, E_DEV))
        earlier = iota((E_DEV, E_DEV), 0) < iota((E_DEV, E_DEV), 1)
        same = jnp.where((across == across.T) & earlier, 1.0, 0.0)
        prior = look_up(counts[...], high, low_f)[0] + jnp.sum(same, axis=0, keepdims=True)
        counts[...] = counts[...] + flat(low, high)
        block, inner = place_of(i * 8 + j)
        once = jnp.where(prior == 0, 1.0, 0.0)
        marks = jnp.concatenate([low_f * (once * block), low_f * (once * inner)])
        firsts[...] = firsts[...] + flat(marks.astype(jnp.bfloat16), high)
        kept.append(prior)
    priors[at, :] = jnp.concatenate(kept)


def list_block(i, ids_ref, state):
    counts, firsts, priors, on_rim, lists, used = state
    bf, f32 = jnp.bfloat16, jnp.float32
    at = pl.ds(pl.multiple_of(i * 8, 8), 8)
    tile, before_it = ids_ref[at, :], priors[at, :]
    for j in range(8):
        high, low = digits(tile[j : j + 1])
        low_f = low.astype(f32)
        prior = before_it[j : j + 1]
        tables = jnp.concatenate([counts[...], on_rim[...], firsts[...]])
        total, rim, rep_block, rep_inner = look_up(tables, high, low_f)
        again = jnp.where(prior > 0, 1.0, 0.0)
        lone = again * jnp.where((total == 2) & (rim == 0), 1.0, 0.0)
        kinds = jnp.concatenate([lone, again - lone, jnp.zeros((6, E_DEV), f32)])
        earlier = iota((E_DEV, E_DEV), 0) < iota((E_DEV, E_DEV), 1)
        before = jnp.dot(
            kinds.astype(bf), jnp.where(earlier, 1.0, 0.0).astype(bf), preferred_element_type=f32
        ) + used[:, 0:1]
        used[...] = used[...] + jnp.sum(kinds, axis=1, keepdims=True)
        slot = jnp.where(lone > 0, before[0:1], LISTED - 1 - before[1:2]).astype(jnp.int32)
        slot_high, slot_low = digits(slot)
        slot_low = slot_low.astype(f32) * again
        block, inner = place_of(i * 8 + j)
        left = jnp.concatenate([slot_low * v for v in (block, inner, rep_block, rep_inner)]).astype(bf)
        lists[...] = lists[...] + flat(left, slot_high)


def lists_start(rim_ref, state):
    for ref in state:
        ref[...] = jnp.zeros_like(ref)
    for k in range(2):
        high, low = digits(rim_ref[0][k : k + 1])
        state[3][...] = state[3][...] + flat(low, high)


def lists_end(rim_ref, state, lists_ref):
    counts, firsts, priors, on_rim, lists, used = state
    index = iota((128, 128), 0) * 128 + iota((128, 128), 1)
    front = used[0:1, 0:1].astype(jnp.int32)
    end = LISTED - used[1:2, 0:1].astype(jnp.int32)
    for k in range(2):
        at = lists[256 * k : 256 * k + 128] * 128.0 + lists[256 * k + 128 : 256 * k + 256]
        filled = (index < front) | (index >= end)
        entries = jnp.where(filled, at.T.astype(jnp.int32), POINTS)
        lists_ref[k * LIST_ROWS : (k + 1) * LIST_ROWS] = jnp.where(index < LISTED, entries, front)[0:LIST_ROWS]
    lists_ref[2 * LIST_ROWS :] = jnp.zeros((8, 128), jnp.int32)
    for k in range(2):
        high, low = digits(rim_ref[0][k : k + 1])
        rep_block, rep_inner = look_up(firsts[...], high, low.astype(jnp.float32))
        at = (rep_block * 128.0 + rep_inner).astype(jnp.int32)
        begin = 2 * LIST_ROWS + 2 * k
        lists_ref[begin : begin + 1] = at[:, 0:128]
        lists_ref[begin + 1 : begin + 2, 0 : RIM - 128] = at[:, 128:RIM]


def assemble_kernel(lists_ref, table_ref, rims_ref, out_ref, table, out, sem, out_sem):
    load = pltpu.make_async_copy(table_ref, table.at[pl.ds(0, POINTS)], sem.at[0])
    load.start()
    table[pl.ds(POINTS, 8)] = jnp.zeros((8, 1, 128), jnp.float32)
    load.wait()
    front = lists_ref[PLACES - 1]

    def entries(first):
        return [lists_ref[first + k] for k in range(BATCH)], [lists_ref[PLACES + first + k] for k in range(BATCH)]

    def pairs(t, _):
        places, reps = entries(t * BATCH)
        vals = [table[reps[k]] + table[places[k]] for k in range(BATCH)]
        for k in range(BATCH):
            table[reps[k]] = vals[k]
            table[places[k]] = vals[k]
        return 0
    lax.fori_loop(0, (front + BATCH - 1) // BATCH, pairs, 0)

    def add(t, _):
        at = lists_ref[PLACES + LISTED - 1 - t]
        table[at] = table[at] + table[lists_ref[LISTED - 1 - t]]
        return 0
    lax.fori_loop(0, EXTRA - front, add, 0)

    def meet(t, _):
        for side in range(2):
            for k in range(9):
                table[lists_ref[2 * PLACES + side * RIM_PAD + t * 9 + k]] = rims_ref[side * RIM_PAD + t * 9 + k]
        return 0
    lax.fori_loop(0, RIM // 9, meet, 0)

    def spread(t, _):
        places, reps = entries(LISTED - BATCH - t * BATCH)
        vals = [table[reps[k]] for k in range(BATCH)]
        for k in range(BATCH):
            table[places[k]] = vals[k]
        return 0
    lax.fori_loop(0, (EXTRA - front + BATCH - 1) // BATCH, spread, 0)

    def block_copy(t):
        at = (
            slice(None),
            pl.ds(pl.multiple_of((t % 8) * 8, 8), 8),
            pl.ds(pl.multiple_of((t // 8) * LANES, LANES), LANES),
        )
        return pltpu.make_async_copy(out.at[at], out_ref.at[at], out_sem.at[t])

    def write(t, _):
        h, i = t // 8, t % 8
        parts = []
        for j in range(8):
            begin = pl.multiple_of((h * NODES + i * 8 + j) * LANES, LANES)
            cols = table[pl.ds(begin, LANES)].reshape(LANES, 128).T
            parts.append(cols[0:48] / cols[48:49])
        block = jnp.swapaxes(jnp.stack(parts), 0, 1)
        out[:, pl.ds(pl.multiple_of(i * 8, 8), 8), pl.ds(pl.multiple_of(h * LANES, LANES), LANES)] = block
        block_copy(t).start()
        return 0
    lax.fori_loop(0, 16, write, 0)

    def written(t, _):
        block_copy(t).wait()
        return 0
    lax.fori_loop(0, 16, written, 0)


def assemble(table, lists, rims):
    smem = pl.BlockSpec(memory_space=pltpu.SMEM)
    vmem = pl.BlockSpec(memory_space=pltpu.VMEM)
    hbm = pl.BlockSpec(memory_space=pl.ANY)
    f32 = jnp.float32
    return pl.pallas_call(
        assemble_kernel,
        out_shape=jax.ShapeDtypeStruct((3 * COEFS, NODES, E_DEV), f32),
        in_specs=[smem, hbm, vmem],
        out_specs=hbm,
        scratch_shapes=[
            pltpu.VMEM((POINTS + 8, 1, 128), f32),
            pltpu.VMEM((3 * COEFS, NODES, E_DEV), f32),
            pltpu.SemaphoreType.DMA((1,)),
            pltpu.SemaphoreType.DMA((16,)),
        ],
        compiler_params=pltpu.CompilerParams(vmem_limit_bytes=VMEM_LIMIT),
        name="assemble",
    )(
        lists.reshape(-1), table.reshape(POINTS, 1, 128), rims.reshape(2 * RIM_PAD, 1, 128),
    )


def body(adj_modes, base_flow, geometry, mass, connect, edge_nodes):
    table, lists, rims = step(adj_modes, base_flow, geometry, mass, connect, edge_nodes)
    return assemble(table, lists, rims).reshape(adj_modes.shape)


def solution(mesh):
    return jax.shard_map(
        body,
        mesh=mesh,
        in_specs=(
            P(None, "four", None, "mesh"),
            P(None, None, "four", "mesh"),
            P(None, None, "mesh"),
            P(None, "mesh"),
            P(None, "mesh"),
            P("mesh", None, None),
        ),
        out_specs=P(None, "four", None, "mesh"),
        check_vma=False,
    )
```

```python
import functools
import math

import jax
import jax.numpy as jnp
import numpy as np
from jax import lax
from jax.experimental import pallas as pl
from jax.experimental.pallas import tpu as pltpu
from jax.sharding import PartitionSpec as P

NP = 8
NODES = 64
PLANES = 256
UNIQUE = 12825
E_DEV = 256
POINTS = NODES * E_DEV
EXTRA = POINTS - UNIQUE
BATCH = 8
LISTED = (EXTRA + BATCH + 127) // 128 * 128
LIST_ROWS = (LISTED // 128 + 8) // 8 * 8
PLACES = LIST_ROWS * 128
RIM = 225
RIM_PAD = 256
HALVES = 2
LANES = E_DEV // HALVES
N_MESH = 16
GROUP = 16
COEFS = PLANES // GROUP
STEP_SIZE = 0.1
HIGH = lax.Precision.HIGHEST
MESH = pl.DeviceIdType.MESH
VMEM_LIMIT = 60 * 2**20


def legendre_values(degree, point):
    before = 1.0
    current = point
    for order in range(1, degree):
        after = ((2 * order + 1) * point * current - order * before) / (order + 1)
        before = current
        current = after
    return (current, before)


def gll_derivative(points_n):
    degree = points_n - 1
    points = []
    for index in range(points_n):
        point = -math.cos(math.pi * index / degree)
        for sweep in range(100):
            top_val, below_val = legendre_values(degree, point)
            point = point - (point * top_val - below_val) / (points_n * top_val)
        points.append(point)
    values = [legendre_values(degree, point)[0] for point in points]
    rows = [
        [
            0.0 if r == c else values[r] / (values[c] * (points[r] - points[c]))
            for c in range(points_n)
        ]
        for r in range(points_n)
    ]
    rows[0][0] = -degree * (degree + 1) / 4.0
    rows[degree][degree] = degree * (degree + 1) / 4.0
    return np.asarray(rows, np.float32)


def plane_tables():
    plane = np.arange(PLANES)
    wave = plane // 2
    phase = (plane[:, None] * wave[None, :] % PLANES) * (2.0 * math.pi / PLANES)
    synth = np.where(plane[None, :] % 2 == 1, np.sin(phase), np.cos(phase))
    synth[:, 1] = 1 - 2 * (plane % 2)
    scales = np.where(wave == 0, 1.0 / PLANES, 2.0 / PLANES)
    analysis = synth.T * scales[:, None]
    number = wave * (2.0 / PLANES)
    axial = np.zeros((PLANES, PLANES))
    axial[plane[::2], plane[1::2]] = number[::2]
    axial[plane[1::2], plane[::2]] = -number[1::2]
    both = np.concatenate([synth, synth @ axial])
    return both.astype(np.float32), (STEP_SIZE * analysis).astype(np.float32)


def step_kernel(
    u_ref, base_ref, geometry_ref, mass_ref, ids_ref, rim_ref, synth_ref, anal_ref,
    table_ref, lists_ref, rims_ref,
    u, ut, along, rows, slopes, base, stage, inputs, fields, forcing, back, returned, table,
    row_send, relay_send, slope_send, back_send, row_recv, slope_recv, back_recv,
    own_sem, stage_sem, table_sem, u_sem, geo, rim_ids, rim_parts, rims, met, rim_send, rim_recv, *lists_state,
):
    deriv = gll_derivative(NP)
    me = lax.axis_index("four")
    x, z = me // 8, me % 8
    odd = z % 2
    sign = 1 - 2 * odd
    partner = x * 8 + z + sign

    def remote(src, dst, send, recv, to):
        return pltpu.make_async_remote_copy(
            src_ref=src, dst_ref=dst, send_sem=send, recv_sem=recv,
            device_id={"four": to}, device_id_type=MESH,
        )

    def source(dx, k):
        return ((x + dx) % 2) * 8 + (z - sign * k + 8) % 8

    def target(dx, k):
        off = (0, 2, -1, -3)[k]
        return ((x + dx) % 2) * 8 + (z + sign * off + 8) % 8

    def pair(dev):
        return pl.multiple_of((dev // 2) * 8, 8)

    def stage_copy(f):
        return pltpu.make_async_copy(base_ref.at[f], stage.at[f % 2], stage_sem.at[f % 2])

    def u_copy(h):
        return pltpu.make_async_copy(u_ref.at[:, :, :, pl.ds(h * LANES, LANES)], u.at[h], u_sem.at[h])

    def turn(h):
        u_copy(h).wait()
        def block(t, _):
            c = t // 8
            i = pl.multiple_of((t % 8) * 8, 8)
            ut[h, c, pl.ds(i, 8)] = jnp.swapaxes(u[h, c, :, pl.ds(i, 8)], 0, 1)
            return 0
        lax.fori_loop(0, 24, block, 0)

    def differentiate(h):
        def block(t, _):
            c, j = t // 8, t % 8
            vals = [ut[h, c, 8 * i + j] for i in range(8)]
            for i in range(8):
                total = vals[0] * float(deriv[i, 0])
                for k in range(1, 8):
                    total = total + vals[k] * float(deriv[i, k])
                along[h, c, 8 * i + j] = total
            return 0
        lax.fori_loop(0, 24, block, 0)

    def u_rows(h, dev):
        return u_ref.at[:, :, pl.ds(pair(dev), 8), pl.ds(h * LANES, LANES)]

    def row_copy(h, dx, k):
        to = target(dx, k)
        return remote(u_rows(h, to), rows.at[h, me], row_send.at[h, dx * 4 + k], row_recv.at[h, me], to)

    def own_relay(h):
        return remote(u_rows(h, me), rows.at[h, me], relay_send.at[h, 0], row_recv.at[h, me], partner)

    def relay(h, dx, k):
        src = source(dx, k)
        return remote(rows.at[h, src], rows.at[h, src], relay_send.at[h, dx * 4 + k], row_recv.at[h, src], partner)

    def far_source(dx, k):
        return ((x + dx) % 2) * 8 + (z + sign + sign * k + 8) % 8

    def row_wait(h, src):
        remote(rows.at[h, src], rows.at[h, src], relay_send.at[h, 0], row_recv.at[h, src], partner).wait_recv()

    def slope_copy(h, t):
        to = (me + t) % GROUP
        return remote(
            along.at[h, :, pl.ds(to * 4, 4)], slopes.at[h, me], slope_send.at[h, t], slope_recv.at[h, me], to
        )

    def slope_wait(h, t):
        src = (me + t) % GROUP
        remote(slopes.at[h, src], slopes.at[h, src], slope_send.at[h, t], slope_recv.at[h, src], src).wait_recv()

    def back_copy(h, g, t):
        to = (me + t) % GROUP
        return remote(
            back.at[h, g, to], returned.at[h, g, me], back_send.at[h, g, t], back_recv.at[h, g, me], to
        )

    def back_wait(h, g, src):
        remote(
            returned.at[h, g, src], returned.at[h, g, src], back_send.at[h, g, 0], back_recv.at[h, g, src], partner
        ).wait_recv()

    def own_copies(h):
        return (
            pltpu.make_async_copy(u_rows(h, me), rows.at[h, me], own_sem.at[h, 0]),
            pltpu.make_async_copy(along.at[h, :, pl.ds(me * 4, 4)], slopes.at[h, me], own_sem.at[h, 1]),
        )

    def own_back(h, g):
        return pltpu.make_async_copy(back.at[h, g, me], returned.at[h, g, me], own_sem.at[h, 2 + g])

    def send_back(h, g):
        own_back(h, g).start()
        each(lambda t: back_copy(h, g, t).start())

    NEAR = [(1, 0), (0, 1), (1, 1), (0, 2), (1, 2), (0, 3), (1, 3)]
    SENT = [(0, 3), (1, 3), (0, 1), (1, 1), (0, 2), (1, 2), (1, 0)]

    def each(fn):
        def go(t, _):
            fn(t)
            return 0
        lax.fori_loop(1, GROUP, go, 0)

    def send_rows(h):
        for dx, k in SENT:
            row_copy(h, dx, k).start()
        own_relay(h).start()

    def send_slopes(h):
        each(lambda t: slope_copy(h, t).start())

    def relays(h):
        for dx, k in NEAR:
            row_wait(h, source(dx, k))
            relay(h, dx, k).start()

    def compute(h, after):
        for copy in own_copies(h):
            copy.wait()
        for k in range(4):
            for dx in range(2):
                row_wait(h, far_source(dx, k))
        each(lambda t: slope_wait(h, t))

        def gather(s, _):
            at = pl.ds(pl.multiple_of(s * COEFS, COEFS), COEFS)
            for c in range(3):
                turned = jnp.swapaxes(rows[h, s, c], 0, 1)
                line = [turned[j] for j in range(8)]
                for n in range(4):
                    total = None
                    for k in range(8):
                        term = line[k] * jnp.where(odd == 1, float(deriv[4 + n, k]), float(deriv[n, k]))
                        total = term if total is None else total + term
                    inputs[n, at, pl.ds(c * LANES, LANES)] = jnp.where(odd == 1, line[4 + n], line[n])
                    inputs[n, at, pl.ds((3 + c) * LANES, LANES)] = total
                    inputs[n, at, pl.ds((6 + c) * LANES, LANES)] = slopes[h, s, c, n]
            return 0
        lax.fori_loop(0, GROUP, gather, 0)

        def node(n, _):
            fields[:, 0 : 9 * LANES] = jnp.dot(
                synth_ref[0:PLANES], inputs[n], precision=HIGH, preferred_element_type=jnp.float32
            )
            fields[:, 9 * LANES : 12 * LANES] = jnp.dot(
                synth_ref[PLANES : 2 * PLANES], inputs[n, :, 0 : 3 * LANES],
                precision=HIGH, preferred_element_type=jnp.float32,
            )
            metric = [geo[g, n, :, pl.ds(h * LANES, LANES)] for g in range(4)]

            def planes(p, _):
                at = pl.ds(pl.multiple_of(p * 16, 16), 16)
                flow = [base[f, n, at, pl.ds(h * LANES, LANES)].astype(jnp.float32) for f in range(12)]
                get = lambda f: fields[at, f * LANES : (f + 1) * LANES]
                on_r = flow[0] * metric[0] + flow[1] * metric[2]
                on_s = flow[0] * metric[1] + flow[1] * metric[3]
                vel = [get(c) for c in range(3)]
                for c in range(3):
                    total = vel[0] * flow[3 + 3 * c] + vel[1] * flow[4 + 3 * c] + vel[2] * flow[5 + 3 * c]
                    total = total - on_r * get(6 + c) - on_s * get(3 + c) - flow[2] * get(9 + c)
                    forcing[at, c * LANES : (c + 1) * LANES] = total
                return 0
            lax.fori_loop(0, PLANES // 16, planes, 0)
            modes = jnp.dot(anal_ref[...], forcing[...], precision=HIGH, preferred_element_type=jnp.float32)
            for c in range(3):
                back[h, n // 2, :, n % 2, c] = modes[:, c * LANES : (c + 1) * LANES].reshape(GROUP, COEFS, LANES)
            return 0
        for g in range(2):
            lax.fori_loop(2 * g, 2 * g + 2, node, 0)
            after(g)

    def table_copy(h, g, s):
        at = pl.ds(pl.multiple_of((h * NODES + 4 * s + 2 * g) * LANES, 2 * LANES), 2 * LANES)
        return pltpu.make_async_copy(table.at[at], table_ref.at[at], table_sem.at[h, g, s])

    def four_rows(block, s):
        return jnp.where(s % 2 == 1, block[4:8], block[0:4])

    def rim_start():
        for k in range(2):
            row = jnp.concatenate([rim_ref[0, k : k + 1], jnp.full((1, RIM_PAD - RIM), -1, jnp.int32)], axis=1)
            rim_ids[k * RIM_PAD : (k + 1) * RIM_PAD] = jnp.broadcast_to(row.astype(jnp.float32), (128, RIM_PAD)).T
        rim_parts[...] = jnp.zeros_like(rim_parts)

    def rim_sums(values, ids):
        pieces = []
        for _ in range(3):
            pieces.append(values.astype(jnp.bfloat16))
            values = values - pieces[-1].astype(jnp.float32)
        hit = jnp.concatenate([(rim_ids[...] == row.astype(jnp.float32)).astype(jnp.bfloat16) for row in ids], axis=1)
        rim_parts[...] = rim_parts[...] + lax.dot_general(
            hit, jnp.concatenate(pieces), (((1,), (1,)), ((), ())), preferred_element_type=jnp.float32
        )

    def rim_total():
        parts = rim_parts[...]
        total = parts[:, 0:64] + (parts[:, 64:128] + parts[:, 128:192])
        rims[...] = jnp.concatenate([total, jnp.zeros_like(total)], axis=1)

    def rim_copy(side):
        to = (lax.axis_index("mesh") + (N_MESH - 1 if side == 0 else 1)) % N_MESH
        return pltpu.make_async_remote_copy(
            src_ref=rims.at[pl.ds(side * RIM_PAD, RIM_PAD)], dst_ref=met.at[pl.ds((1 - side) * RIM_PAD, RIM_PAD)],
            send_sem=rim_send.at[side], recv_sem=rim_recv.at[1 - side],
            device_id={"mesh": to}, device_id_type=MESH,
        )

    def finish(h, g, s):
        tile = pl.ds(pl.multiple_of((s // 2) * 8, 8), 8)
        half = pl.ds(h * LANES, LANES)
        weights = four_rows(mass_ref[tile, half], s)
        ids = four_rows(ids_ref[tile, half], s)
        tall = []
        for n in range(2):
            at = 4 * s + 2 * g + n
            weight = weights[2 * g + n : 2 * g + n + 1]
            parts = [(ut[h, c, at] + returned[h, g, s, n, c]) * weight for c in range(3)]
            parts.append(jnp.broadcast_to(weight, (8, LANES)))
            parts.append(jnp.zeros((8, LANES), jnp.float32))
            tall.append(jnp.concatenate(parts))
            begin = pl.multiple_of((h * NODES + at) * LANES, LANES)
            table[pl.ds(begin, LANES)] = jnp.concatenate([tall[-1], jnp.zeros((64, LANES), jnp.float32)]).T
        table_copy(h, g, s).start()
        rim_sums(jnp.concatenate(tall, axis=1), [ids[2 * g + n : 2 * g + n + 1] for n in range(2)])

    def lists_part(block):
        def go(i, _):
            block(i, ids_ref, lists_state)
            return 0
        lax.fori_loop(0, NODES // 8, go, 0)

    for h in range(HALVES):
        u_copy(h).start()
    barrier = pltpu.get_barrier_semaphore()
    each(lambda t: pl.semaphore_signal(barrier, inc=1, device_id={"four": (me + t) % GROUP}, device_id_type=MESH))
    for off in (1, N_MESH - 1):
        pl.semaphore_signal(
            barrier, inc=1, device_id={"mesh": (lax.axis_index("mesh") + off) % N_MESH}, device_id_type=MESH
        )
    pl.semaphore_wait(barrier, GROUP + 1)
    send_rows(0)
    turn(0)
    differentiate(0)
    send_slopes(0)
    for copy in own_copies(0):
        copy.start()
    stage_copy(0).start()
    stage_copy(1).start()
    turn(1)
    differentiate(1)
    for copy in own_copies(1):
        copy.start()

    for f in range(12):
        stage_copy(f).wait()

        def move(t, _):
            p = pl.multiple_of(t * 64, 64)
            block = stage[f % 2, pl.ds(p, 64)].astype(jnp.float32)
            base[f, :, pl.ds(p, 64), :] = jnp.swapaxes(block, 0, 1).astype(jnp.bfloat16)
            return 0
        lax.fori_loop(0, 4, move, 0)
        if f + 2 < 12:
            stage_copy(f + 2).start()

    for g in range(4):
        own = four_rows(geometry_ref[g, pl.ds(pair(me), 8), :], me)
        for n in range(4):
            geo[g, n] = own[n : n + 1]

    relays(0)
    send_rows(1)
    send_slopes(1)
    lists_start(rim_ref, lists_state)
    rim_start()
    lists_part(count_block)
    compute(0, lambda g: None)
    relays(1)
    for g in range(2):
        send_back(0, g)
    lists_part(list_block)
    lists_end(rim_ref, lists_state, lists_ref)
    compute(1, lambda g: send_back(1, g))

    for h in range(HALVES):
        for dx, k in SENT:
            row_copy(h, dx, k).wait_send()
        own_relay(h).wait_send()
        for dx, k in NEAR:
            relay(h, dx, k).wait_send()
        each(lambda t: slope_copy(h, t).wait_send())

    def returns_sent(h):
        for g in range(2):
            each(lambda t: back_copy(h, g, t).wait_send())

            def drained(s, _):
                table_copy(h, g, s).wait()
                return 0
            lax.fori_loop(0, GROUP, drained, 0)

    for h in range(HALVES):
        if h == 1:
            returns_sent(0)
        for g in range(2):
            own_back(h, g).wait()
            finish(h, g, me)

            def arrive(t, _):
                src = (me + t) % GROUP
                back_wait(h, g, src)
                finish(h, g, src)
                return 0
            lax.fori_loop(1, GROUP, arrive, 0)
    rim_total()

    for side in range(2):
        rim_copy(side).start()
    returns_sent(1)
    for side in range(2):
        rim_copy(side).wait_recv()
        rim_copy(side).wait_send()
    rims_ref[...] = rims[...] + met[...]


def step(u, base, geometry, mass, ids, rim):
    synth, anal = plane_tables()
    vmem = pl.BlockSpec(memory_space=pltpu.VMEM)
    hbm = pl.BlockSpec(memory_space=pl.ANY)
    f32 = jnp.float32
    dma = pltpu.SemaphoreType.DMA
    return pl.pallas_call(
        step_kernel,
        out_shape=(
            jax.ShapeDtypeStruct((POINTS, 128), f32),
            jax.ShapeDtypeStruct((2 * LIST_ROWS + 8, 128), jnp.int32),
            jax.ShapeDtypeStruct((2 * RIM_PAD, 128), f32),
        ),
        in_specs=[hbm, hbm] + [vmem] * 6,
        out_specs=(hbm, vmem, vmem),
        scratch_shapes=[
            pltpu.VMEM((HALVES, 3, COEFS, NODES, LANES), f32),
            pltpu.VMEM((HALVES, 3, NODES, COEFS, LANES), f32),
            pltpu.VMEM((HALVES, 3, NODES, COEFS, LANES), f32),
            pltpu.VMEM((HALVES, GROUP, 3, COEFS, 8, LANES), f32),
            pltpu.VMEM((HALVES, GROUP, 3, 4, COEFS, LANES), f32),
            pltpu.VMEM((12, 4, PLANES, E_DEV), jnp.bfloat16),
            pltpu.VMEM((2, PLANES, 4, E_DEV), jnp.bfloat16),
            pltpu.VMEM((4, PLANES, 9 * LANES), f32),
            pltpu.VMEM((PLANES, 12 * LANES), f32),
            pltpu.VMEM((PLANES, 3 * LANES), f32),
            pltpu.VMEM((HALVES, 2, GROUP, 2, 3, COEFS, LANES), f32),
            pltpu.VMEM((HALVES, 2, GROUP, 2, 3, COEFS, LANES), f32),
            pltpu.VMEM((POINTS, 128), f32),
            dma((HALVES, 8)), dma((HALVES, 8)), dma((HALVES, GROUP)), dma((HALVES, 2, GROUP)),
            dma((HALVES, GROUP)), dma((HALVES, GROUP)), dma((HALVES, 2, GROUP)),
            dma((HALVES, 4)), dma((2,)), dma((HALVES, 2, GROUP)),
            dma((HALVES,)),
            pltpu.VMEM((4, 4, 1, E_DEV), f32),
            pltpu.VMEM((2 * RIM_PAD, 128), f32),
            pltpu.VMEM((2 * RIM_PAD, 192), f32),
            pltpu.VMEM((2 * RIM_PAD, 128), f32),
            pltpu.VMEM((2 * RIM_PAD, 128), f32),
            dma((2,)), dma((2,)),
            pltpu.VMEM((128, 128), f32),
            pltpu.VMEM((256, 128), f32),
            pltpu.VMEM((NODES, E_DEV), f32),
            pltpu.VMEM((128, 128), f32),
            pltpu.VMEM((512, 128), f32),
            pltpu.VMEM((8, 128), f32),
        ],
        compiler_params=pltpu.CompilerParams(
            collective_id=0, has_side_effects=True, vmem_limit_bytes=VMEM_LIMIT
        ),
        name="step",
    )(u, base, geometry, mass, ids, rim, jnp.asarray(synth), jnp.asarray(anal))


def iota(shape, dim):
    return lax.broadcasted_iota(jnp.int32, shape, dim)


def flat(left, right):
    return lax.dot_general(left, right, (((1,), (1,)), ((), ())), preferred_element_type=jnp.float32)


def digits(ids):
    digit = iota((128, ids.shape[1]), 0)
    return (digit == ids // 128).astype(jnp.bfloat16), (digit == ids % 128).astype(jnp.bfloat16)


def look_up(tables, high, low):
    found = jnp.dot(tables.astype(jnp.bfloat16), high, preferred_element_type=jnp.float32)
    return [
        jnp.sum(found[k : k + 128] * low, axis=0, keepdims=True) for k in range(0, tables.shape[0], 128)
    ]


def place_of(n):
    lane = iota((1, E_DEV), 1)
    return ((lane // LANES) * NODES + n).astype(jnp.float32), (lane % LANES).astype(jnp.float32)


def count_block(i, ids_ref, state):
    counts, firsts, priors = state[0], state[1], state[2]
    at = pl.ds(pl.multiple_of(i * 8, 8), 8)
    tile = ids_ref[at, :]
    kept = []
    for j in range(8):
        ids = tile[j : j + 1]
        high, low = digits(ids)
        low_f = low.astype(jnp.float32)
        across = jnp.broadcast_to(ids.astype(jnp.float32), (E_DEV, E_DEV))
        earlier = iota((E_DEV, E_DEV), 0) < iota((E_DEV, E_DEV), 1)
        same = jnp.where((across == across.T) & earlier, 1.0, 0.0)
        prior = look_up(counts[...], high, low_f)[0] + jnp.sum(same, axis=0, keepdims=True)
        counts[...] = counts[...] + flat(low, high)
        block, inner = place_of(i * 8 + j)
        once = jnp.where(prior == 0, 1.0, 0.0)
        marks = jnp.concatenate([low_f * (once * block), low_f * (once * inner)])
        firsts[...] = firsts[...] + flat(marks.astype(jnp.bfloat16), high)
        kept.append(prior)
    priors[at, :] = jnp.concatenate(kept)


def list_block(i, ids_ref, state):
    counts, firsts, priors, on_rim, lists, used = state
    bf, f32 = jnp.bfloat16, jnp.float32
    at = pl.ds(pl.multiple_of(i * 8, 8), 8)
    tile, before_it = ids_ref[at, :], priors[at, :]
    for j in range(8):
        high, low = digits(tile[j : j + 1])
        low_f = low.astype(f32)
        prior = before_it[j : j + 1]
        tables = jnp.concatenate([counts[...], on_rim[...], firsts[...]])
        total, rim, rep_block, rep_inner = look_up(tables, high, low_f)
        again = jnp.where(prior > 0, 1.0, 0.0)
        lone = again * jnp.where((total == 2) & (rim == 0), 1.0, 0.0)
        kinds = jnp.concatenate([lone, again - lone, jnp.zeros((6, E_DEV), f32)])
        earlier = iota((E_DEV, E_DEV), 0) < iota((E_DEV, E_DEV), 1)
        before = jnp.dot(
            kinds.astype(bf), jnp.where(earlier, 1.0, 0.0).astype(bf), preferred_element_type=f32
        ) + used[:, 0:1]
        used[...] = used[...] + jnp.sum(kinds, axis=1, keepdims=True)
        slot = jnp.where(lone > 0, before[0:1], LISTED - 1 - before[1:2]).astype(jnp.int32)
        slot_high, slot_low = digits(slot)
        slot_low = slot_low.astype(f32) * again
        block, inner = place_of(i * 8 + j)
        left = jnp.concatenate([slot_low * v for v in (block, inner, rep_block, rep_inner)]).astype(bf)
        lists[...] = lists[...] + flat(left, slot_high)


def lists_start(rim_ref, state):
    for ref in state:
        ref[...] = jnp.zeros_like(ref)
    for k in range(2):
        high, low = digits(rim_ref[0][k : k + 1])
        state[3][...] = state[3][...] + flat(low, high)


def lists_end(rim_ref, state, lists_ref):
    counts, firsts, priors, on_rim, lists, used = state
    index = iota((128, 128), 0) * 128 + iota((128, 128), 1)
    front = used[0:1, 0:1].astype(jnp.int32)
    end = LISTED - used[1:2, 0:1].astype(jnp.int32)
    for k in range(2):
        at = lists[256 * k : 256 * k + 128] * 128.0 + lists[256 * k + 128 : 256 * k + 256]
        filled = (index < front) | (index >= end)
        entries = jnp.where(filled, at.T.astype(jnp.int32), POINTS)
        lists_ref[k * LIST_ROWS : (k + 1) * LIST_ROWS] = jnp.where(index < LISTED, entries, front)[0:LIST_ROWS]
    lists_ref[2 * LIST_ROWS :] = jnp.zeros((8, 128), jnp.int32)
    for k in range(2):
        high, low = digits(rim_ref[0][k : k + 1])
        rep_block, rep_inner = look_up(firsts[...], high, low.astype(jnp.float32))
        at = (rep_block * 128.0 + rep_inner).astype(jnp.int32)
        begin = 2 * LIST_ROWS + 2 * k
        lists_ref[begin : begin + 1] = at[:, 0:128]
        lists_ref[begin + 1 : begin + 2, 0 : RIM - 128] = at[:, 128:RIM]


def assemble_kernel(lists_ref, table_ref, rims_ref, out_ref, table, out, sem, out_sem):
    load = pltpu.make_async_copy(table_ref, table.at[pl.ds(0, POINTS)], sem.at[0])
    load.start()
    table[pl.ds(POINTS, 8)] = jnp.zeros((8, 1, 128), jnp.float32)
    load.wait()
    front = lists_ref[PLACES - 1]

    def entries(first):
        return [lists_ref[first + k] for k in range(BATCH)], [lists_ref[PLACES + first + k] for k in range(BATCH)]

    def pairs(t, _):
        places, reps = entries(t * BATCH)
        vals = [table[reps[k]] + table[places[k]] for k in range(BATCH)]
        for k in range(BATCH):
            table[reps[k]] = vals[k]
            table[places[k]] = vals[k]
        return 0
    lax.fori_loop(0, (front + BATCH - 1) // BATCH, pairs, 0)

    def add(t, _):
        places, reps = entries(LISTED - BATCH - t * BATCH)
        vals = [table[places[k]] for k in range(BATCH)]
        for k in range(BATCH):
            table[reps[k]] = table[reps[k]] + vals[k]
        return 0
    lax.fori_loop(0, (EXTRA - front + BATCH - 1) // BATCH, add, 0)

    def meet(t, _):
        for side in range(2):
            for k in range(9):
                table[lists_ref[2 * PLACES + side * RIM_PAD + t * 9 + k]] = rims_ref[side * RIM_PAD + t * 9 + k]
        return 0
    lax.fori_loop(0, RIM // 9, meet, 0)

    def spread(t, _):
        places, reps = entries(LISTED - BATCH - t * BATCH)
        vals = [table[reps[k]] for k in range(BATCH)]
        for k in range(BATCH):
            table[places[k]] = vals[k]
        return 0
    lax.fori_loop(0, (EXTRA - front + BATCH - 1) // BATCH, spread, 0)

    def block_copy(t):
        at = (
            slice(None),
            pl.ds(pl.multiple_of((t % 8) * 8, 8), 8),
            pl.ds(pl.multiple_of((t // 8) * LANES, LANES), LANES),
        )
        return pltpu.make_async_copy(out.at[at], out_ref.at[at], out_sem.at[t])

    def write(t, _):
        h, i = t // 8, t % 8
        parts = []
        for j in range(8):
            begin = pl.multiple_of((h * NODES + i * 8 + j) * LANES, LANES)
            cols = table[pl.ds(begin, LANES)].reshape(LANES, 128).T
            parts.append(cols[0:48] / cols[48:49])
        block = jnp.swapaxes(jnp.stack(parts), 0, 1)
        out[:, pl.ds(pl.multiple_of(i * 8, 8), 8), pl.ds(pl.multiple_of(h * LANES, LANES), LANES)] = block
        block_copy(t).start()
        return 0
    lax.fori_loop(0, 16, write, 0)

    def written(t, _):
        block_copy(t).wait()
        return 0
    lax.fori_loop(0, 16, written, 0)


def assemble(table, lists, rims):
    smem = pl.BlockSpec(memory_space=pltpu.SMEM)
    vmem = pl.BlockSpec(memory_space=pltpu.VMEM)
    hbm = pl.BlockSpec(memory_space=pl.ANY)
    f32 = jnp.float32
    return pl.pallas_call(
        assemble_kernel,
        out_shape=jax.ShapeDtypeStruct((3 * COEFS, NODES, E_DEV), f32),
        in_specs=[smem, hbm, vmem],
        out_specs=hbm,
        scratch_shapes=[
            pltpu.VMEM((POINTS + 8, 1, 128), f32),
            pltpu.VMEM((3 * COEFS, NODES, E_DEV), f32),
            pltpu.SemaphoreType.DMA((1,)),
            pltpu.SemaphoreType.DMA((16,)),
        ],
        compiler_params=pltpu.CompilerParams(vmem_limit_bytes=VMEM_LIMIT),
        name="assemble",
    )(
        lists.reshape(-1), table.reshape(POINTS, 1, 128), rims.reshape(2 * RIM_PAD, 1, 128),
    )


def body(adj_modes, base_flow, geometry, mass, connect, edge_nodes):
    table, lists, rims = step(adj_modes, base_flow, geometry, mass, connect, edge_nodes)
    return assemble(table, lists, rims).reshape(adj_modes.shape)


def solution(mesh):
    return jax.shard_map(
        body,
        mesh=mesh,
        in_specs=(
            P(None, "four", None, "mesh"),
            P(None, None, "four", "mesh"),
            P(None, None, "mesh"),
            P(None, "mesh"),
            P(None, "mesh"),
            P("mesh", None, None),
        ),
        out_specs=P(None, "four", None, "mesh"),
        check_vma=False,
    )
```
